256 devices in a mesh: dp: 16 (over x, y_hi, core), space: 16 (over z, y_lo).
Axes of the slice: x: 4, y: 4 (y_hi: 2, y_lo: 2; y = y_hi * 2 + y_lo), z: 8, core: 2. Of those that a mesh axis runs over, the one named last changes fastest.
Arguments:
- fine_map: bfloat16 [256, 80, 32, 128], P('dp', None, 'space'), may hold values from -6 to 6
- coarse_map: bfloat16 [256, 224, 16, 64], P('dp', None, 'space'), may hold values from -6 to 6
- fine_cotan: bfloat16 [256, 384, 32, 128], P('dp', None, 'space'), may hold values from -0.005859375 to 0.005859375
- coarse_cotan: bfloat16 [256, 384, 16, 64], P(('dp', 'space')), may hold values from -0.01171875 to 0.01171875
- lateral_fine: bfloat16 [80, 384], replicated, may hold values from -0.625 to 0.625
- lateral_coarse: bfloat16 [224, 384], replicated, may hold values from -0.375 to 0.375
- point_fine: bfloat16 [384, 384], replicated, may hold values from -0.3125 to 0.3125
- point_coarse: bfloat16 [384, 384], replicated, may hold values from -0.3125 to 0.3125
- kernel_fine: float32 [3, 3, 384], replicated, may hold values from -2 to 2
- kernel_coarse: float32 [3, 3, 384], replicated, may hold values from -2 to 2
- joining: float32 [4], replicated, may hold values from 0.5 to 2
Outputs:
- grad_lateral_fine: float32 [80, 384], replicated
- grad_lateral_coarse: float32 [224, 384], replicated
- grad_point_fine: float32 [384, 384], replicated
- grad_point_coarse: float32 [384, 384], replicated
- grad_kernel_fine: float32 [3, 3, 384], replicated
- grad_kernel_coarse: float32 [3, 3, 384], replicated
- grad_joining: float32 [4], replicated
The draws below stay inside these ranges and needn't reach their ends.
All inputs are finite; a program needn't handle non-finite values.
Results may differ from the reference program's by a relative error of at most 0.025.
Values may be sent and summed in bfloat16 or wider, within the bound.
No kernel may reach another device: no remote copies, remote signals or barrier semaphores. Data moves between devices by JAX's collectives and lax.ppermute only.
A program may use at most 128 MiB of HBM per device.

```python
import math
import jax
import jax.numpy as jnp
from jax import lax

F = 384
C3 = 80
C4 = 224
BATCH = 256
H3 = 32
W3 = 128
H4 = 16
W4 = 64


def shard_levels(rng, extent, split, low, high):
    def one(axis_at, blocks):
        draws = jax.random.uniform(jax.random.fold_in(jax.random.fold_in(rng, 6), axis_at), (blocks,), jnp.float32, low / len(split), high / len(split))
        return jnp.repeat(jnp.exp(draws), extent[axis_at] // blocks).reshape((-1,) + (1,) * (len(extent) - axis_at - 1))

    factor_of = one(*split[0])
    for cut in split[1:]:
        factor_of = factor_of * one(*cut)
    return factor_of


def scatter_about(key, extent, deviation, reach, pieces=(), kind=jnp.bfloat16):
    loudness = shard_levels(key, extent, pieces, -0.22, 0.18) if pieces else 1.0
    result = jax.random.normal(key, extent, jnp.float32) * deviation * loudness
    return jnp.minimum(jnp.maximum(result, -reach), reach).astype(kind)


def setup_inputs(seed: int = 0) -> dict:
    key_list = jax.random.split(jax.random.key(seed), 12)
    return {
        "fine_map": scatter_about(key_list[0], (BATCH, C3, H3, W3), 1.0, 6.0, ((0, 16), (2, 16))),
        "coarse_map": scatter_about(key_list[1], (BATCH, C4, H4, W4), 1.0, 6.0, ((0, 16), (2, 16))),
        "fine_cotan": scatter_about(key_list[2], (BATCH, F, H3, W3), (1.0 / (BATCH * H3 * W3) ** 0.5), 0.005859375, ((0, 16), (2, 16))),
        "coarse_cotan": scatter_about(key_list[3], (BATCH, F, H4, W4), (1.0 / (BATCH * H4 * W4) ** 0.5), 0.01171875, ((0, 256),)),
        "lateral_fine": scatter_about(key_list[4], (C3, F), C3 ** -0.5, 0.625),
        "lateral_coarse": scatter_about(key_list[5], (C4, F), C4 ** -0.5, 0.375),
        "point_fine": scatter_about(key_list[6], (F, F), F ** -0.5, 0.3125),
        "point_coarse": scatter_about(key_list[7], (F, F), F ** -0.5, 0.3125),
        "kernel_fine": scatter_about(key_list[8], (3, 3, F), 9 ** -0.5, 2.0, (), jnp.float32),
        "kernel_coarse": scatter_about(key_list[9], (3, 3, F), 9 ** -0.5, 2.0, (), jnp.float32),
        "joining": jnp.clip(jnp.exp(jax.random.uniform(key_list[10], (4,), jnp.float32, math.log(0.5), math.log(2.0))), 0.5, 2.0),
    }


EPSILON = 0.0001

def swish(values):
    return values * jax.nn.sigmoid(values)

def swish_slope(values):
    logistic = jax.nn.sigmoid(values)
    return logistic * (1.0 + values * (1.0 - logistic))

def project(weight, values):
    return jnp.einsum('cf,bcrw->bfrw', weight.astype(jnp.float32), values.astype(jnp.float32))

def project_back(weight, cotangent):
    return jnp.einsum('cf,bfrw->bcrw', weight.astype(jnp.float32), cotangent.astype(jnp.float32))

def weight_grad(values, cotangent):
    return jnp.einsum('bcrw,bfrw->cf', values.astype(jnp.float32), cotangent.astype(jnp.float32))

def upsample(values):
    return jnp.repeat(jnp.repeat(values, 2, axis=2), 2, axis=3)

def pool_sum(values):
    shaped = values.reshape(values.shape[0], values.shape[1], values.shape[2] // 2, 2, values.shape[3] // 2, 2)
    return shaped.sum(axis=(3, 5))

def zero_rows(values):
    return jnp.pad(values, ((0, 0), (0, 0), (1, 1), (0, 0)))

def widen(padded):
    return jnp.pad(padded, ((0, 0), (0, 0), (0, 0), (1, 1))).astype(jnp.float32)

def spread(padded, kernel, reverse):
    row_count = padded.shape[2] - 2
    col_count = padded.shape[3]
    widened = widen(padded)
    running = jnp.zeros((padded.shape[0], padded.shape[1], row_count, col_count), jnp.float32)
    for row_off in range(3):
        for col_off in range(3):
            row_start = 2 - row_off if reverse else row_off
            col_start = 2 - col_off if reverse else col_off
            running = running + kernel[row_off, col_off][None, :, None, None] * widened[:, :, row_start:row_start + row_count, col_start:col_start + col_count]
    return running

def kernel_grad(cotangent, padded):
    row_count = padded.shape[2] - 2
    col_count = padded.shape[3]
    widened = widen(padded)
    cotangent_wide = cotangent.astype(jnp.float32)
    stacked = []
    for row_off in range(3):
        row_list = []
        for col_off in range(3):
            row_list.append(lax.optimization_barrier(jnp.sum(cotangent_wide * widened[:, :, row_off:row_off + row_count, col_off:col_off + col_count], axis=(0, 2, 3))))
        stacked.append(jnp.stack(row_list))
    return jnp.stack(stacked)

def window_grads(fine_map, coarse_map, fine_cotan, coarse_cotan, lateral_fine, lateral_coarse, point_fine, point_coarse, kernel_fine, kernel_coarse, joining):
    halves = jnp.bfloat16
    floats = jnp.float32
    fine_own, fine_up, coarse_own, coarse_down = (joining[0], joining[1], joining[2], joining[3])
    fine_total = fine_own + fine_up + EPSILON
    coarse_total = coarse_own + coarse_down + EPSILON
    proj_fine = project(lateral_fine, fine_map).astype(halves)
    proj_coarse = project(lateral_coarse, coarse_map).astype(halves)
    upsampled = upsample(proj_coarse)
    joined_fine = (fine_own * proj_fine.astype(floats) + fine_up * upsampled.astype(floats)) / fine_total
    active_fine = swish(joined_fine).astype(halves)
    padded_fine = zero_rows(active_fine)
    depth_fine = spread(padded_fine, kernel_fine, False).astype(halves)
    output_fine = project(point_fine, depth_fine).astype(halves)
    pooled_fine = (0.25 * pool_sum(output_fine.astype(floats))).astype(halves)
    joined_coarse = (coarse_own * proj_coarse.astype(floats) + coarse_down * pooled_fine.astype(floats)) / coarse_total
    active_coarse = swish(joined_coarse).astype(halves)
    padded_coarse = zero_rows(active_coarse)
    depth_coarse = spread(padded_coarse, kernel_coarse, False).astype(halves)
    point_coarse_grad = weight_grad(depth_coarse, coarse_cotan)
    back_coarse = project_back(point_coarse, coarse_cotan).astype(halves)
    kernel_coarse_grad = kernel_grad(back_coarse, padded_coarse)
    slope_coarse = spread(zero_rows(back_coarse), kernel_coarse, True) * swish_slope(joined_coarse)
    own_coarse_grad = jnp.sum(slope_coarse * (proj_coarse.astype(floats) - joined_coarse)) / coarse_total
    down_coarse_grad = jnp.sum(slope_coarse * (pooled_fine.astype(floats) - joined_coarse)) / coarse_total
    pooled_back = (coarse_down / coarse_total * slope_coarse).astype(halves)
    own_back = (coarse_own / coarse_total * slope_coarse).astype(halves)
    mixed_cotan = (fine_cotan.astype(floats) + 0.25 * upsample(pooled_back).astype(floats)).astype(halves)
    point_fine_grad = weight_grad(depth_fine, mixed_cotan)
    back_fine = project_back(point_fine, mixed_cotan).astype(halves)
    kernel_fine_grad = kernel_grad(back_fine, padded_fine)
    slope_fine = spread(zero_rows(back_fine), kernel_fine, True) * swish_slope(joined_fine)
    own_fine_grad = jnp.sum(slope_fine * (proj_fine.astype(floats) - joined_fine)) / fine_total
    up_fine_grad = jnp.sum(slope_fine * (upsampled.astype(floats) - joined_fine)) / fine_total
    lateral_back = (fine_own / fine_total * slope_fine).astype(halves)
    lateral_fine_grad = weight_grad(fine_map, lateral_back)
    up_back = (fine_up / fine_total * pool_sum(slope_fine)).astype(halves)
    lateral_coarse_grad = weight_grad(coarse_map, own_back) + weight_grad(coarse_map, up_back)
    joining_grad = jnp.stack([own_fine_grad, up_fine_grad, own_coarse_grad, down_coarse_grad])
    return (lateral_fine_grad, lateral_coarse_grad, point_fine_grad, point_coarse_grad, kernel_fine_grad, kernel_coarse_grad, joining_grad)

def reference(fine_map, coarse_map, fine_cotan, coarse_cotan, lateral_fine, lateral_coarse, point_fine, point_coarse, kernel_fine, kernel_coarse, joining):

    def per_image(carried, slices):
        terms = window_grads(slices[0][None], slices[1][None], slices[2][None], slices[3][None], lateral_fine, lateral_coarse, point_fine, point_coarse, kernel_fine, kernel_coarse, joining)
        return (tuple((left + right for left, right in zip(carried, terms))), None)
    start = (jnp.zeros((C3, F), jnp.float32), jnp.zeros((C4, F), jnp.float32), jnp.zeros((F, F), jnp.float32), jnp.zeros((F, F), jnp.float32), jnp.zeros((3, 3, F), jnp.float32), jnp.zeros((3, 3, F), jnp.float32), jnp.zeros((4,), jnp.float32))
    summed, _ = lax.scan(per_image, start, (fine_map, coarse_map, fine_cotan, coarse_cotan))
    return (summed[0], summed[1], summed[2], summed[3], summed[4], summed[5], summed[6])
```

```python
import jax
import jax.numpy as jnp
import numpy as np
from jax import lax
from jax.experimental import pallas as pl
from jax.experimental.pallas import tpu as pltpu
from jax.sharding import PartitionSpec as P

EPSILON = 0.0001
F = 384
FB = 128
CH = 16
ROWS = 32
PAIRS = 8
HALF = jnp.bfloat16
WIDE = jnp.float32
ALL = ("dp", "space")
LIMIT = 50 * 1024 * 1024


def nn(left, right):
    return lax.dot_general(left, right, (((1,), (0,)), ((), ())), preferred_element_type=WIDE)


def nt(left, right):
    return lax.dot_general(left, right, (((1,), (1,)), ((), ())), preferred_element_type=WIDE)


def upsampler():
    out = np.zeros((128, 256), np.float32)
    for col in range(128):
        out[col, 2 * col] = 1.0
        out[col, 2 * col + 1] = 1.0
    return out


def upsampler_rows():
    one = upsampler()
    out = np.zeros((2, 128, 256), np.float32)
    for odd in range(2):
        half = one[:, 128 * odd : 128 * odd + 128]
        out[odd, :, :128] = half
        out[odd, :, 128:] = half
    return out


def pooler(scale):
    one = upsampler()
    out = np.zeros((512, 128), np.float32)
    for row in range(4):
        out[128 * row : 128 * row + 128] = one[:, 128 * (row // 2) : 128 * (row // 2) + 128].T
    return out * scale


def lanes(shape):
    return lax.broadcasted_iota(jnp.int32, shape, 1)


def side_fine(cells, lane):
    before = jnp.where(lane == 0, 0.0, pltpu.roll(cells, 1, 1))
    after = jnp.where(lane == 127, 0.0, pltpu.roll(cells, 127, 1))
    return before, cells, after


def side_coarse(cells, lane):
    before = jnp.where((lane % 64) == 0, 0.0, pltpu.roll(cells, 1, 1))
    after = jnp.where((lane % 64) == 63, 0.0, pltpu.roll(cells, 127, 1))
    return before, cells, after


def taps_of(ref, start):
    return [
        [
            jnp.broadcast_to(ref[pl.ds(start, CH), 3 * u + v : 3 * u + v + 1], (CH, 128))
            for v in range(3)
        ]
        for u in range(3)
    ]


def lane_sum(values):
    return jnp.sum(values, axis=1, keepdims=True)


def sigmoid(values):
    return 1.0 / (1.0 + jnp.exp(-values))


def forward_kernel(
    coef, fine, coarse, lat_fine, lat_coarse, kern, up, pool,
    act_out, slope_out, depth_out, proj_out, pooled_out, proj, lifted,
):
    lifted_low = nt(lat_coarse[...], coarse[...]).astype(HALF)
    for k in range(PAIRS):
        pair = lifted_low[:, 128 * k : 128 * k + 128]
        proj_out[k] = pair
        both = nn(pair, up[...])
        lifted[2 * k] = both[:, :128]
        lifted[2 * k + 1] = both[:, 128:]
    for s in range(ROWS // 2):
        both = nn(lat_fine[...], jnp.concatenate([fine[2 * s], fine[2 * s + 1]], axis=1))
        proj[2 * s] = both[:, :128]
        proj[2 * s + 1] = both[:, 128:]
    own, above = coef[0], coef[1]

    @pl.loop(0, FB // CH)
    def _(step):
        start = pl.multiple_of(step * CH, CH)
        at = pl.ds(start, CH)
        taps = taps_of(kern, start)
        lane = lanes((CH, 128))
        sides = {}
        for r in range(ROWS + 1):
            if r < ROWS:
                joined = own * proj[r, at, :] + above * lifted[r // 2, at, :]
                gate = sigmoid(joined)
                active = joined * gate
                act_out[r, at, :] = active.astype(HALF)
                slope_out[r, at, :] = (gate * (1.0 + joined * (1.0 - gate))).astype(HALF)
                sides[r] = side_fine(active, lane)
            if r >= 1:
                total = None
                for u in range(3):
                    if r - 2 + u not in sides:
                        continue
                    for v in range(3):
                        term = taps[u][v] * sides[r - 2 + u][v]
                        total = term if total is None else total + term
                depth_out[r - 1, at, :] = total.astype(HALF)
                sides.pop(r - 2, None)

    for k in range(PAIRS):
        four = jnp.concatenate([depth_out[4 * k + a] for a in range(4)], axis=1)
        pooled_out[k] = nn(four, pool[...]).astype(HALF)


def coarse_kernel(
    coef, pooled_depth, proj, point_fine, point_fine_t, point_coarse, cotan, coarse, kern,
    grad_point, grad_kern, grad_point_fine, quarter_back, grad_lat, sums,
    pooled, active_s, gate_s, back_s, depth_s, pooled_back, own_back,
):
    own, down, scale_own, scale_down = coef[2], coef[3], coef[4], coef[5]
    for k in range(PAIRS):
        pooled[k] = nn(point_fine_t[...], pooled_depth[k]).astype(HALF).astype(WIDE)
        back_s[k] = nt(point_coarse[...], cotan[k]).astype(HALF).astype(WIDE)
    sums[...] = jnp.zeros_like(sums)

    def rows_of(cells, lane):
        turned = [pltpu.roll(c, 64, 1) for c in cells]
        low = lane < 64
        nil = jnp.zeros((CH, 128), WIDE)
        out = []
        for k in range(PAIRS):
            above = jnp.where(low, turned[k - 1] if k else nil, turned[k])
            below = jnp.where(low, turned[k], turned[k + 1] if k + 1 < PAIRS else nil)
            out.append([side_coarse(c, lane) for c in (above, cells[k], below)])
        return out

    @pl.loop(0, F // CH)
    def _(step):
        start = pl.multiple_of(step * CH, CH)
        at = pl.ds(start, CH)
        taps = taps_of(kern, start)
        lane = lanes((CH, 128))
        active, steep = [], []
        for k in range(PAIRS):
            joined = own * proj[k, at, :].astype(WIDE) + down * pooled[k, at, :]
            gate = sigmoid(joined)
            active.append(joined * gate)
            gate_s[k, at, :] = gate * (1.0 + joined * (1.0 - gate))
        near = rows_of(active, lane)
        for k in range(PAIRS):
            active_s[k, at, :] = active[k]
            total = None
            for u in range(3):
                for v in range(3):
                    term = taps[u][v] * near[k][u][v]
                    total = term if total is None else total + term
            depth_s[k, at, :] = total.astype(HALF)

    @pl.loop(0, F // CH)
    def _(step):
        start = pl.multiple_of(step * CH, CH)
        at = pl.ds(start, CH)
        taps = taps_of(kern, start)
        lane = lanes((CH, 128))
        near = rows_of([back_s[k, at, :] for k in range(PAIRS)], lane)
        weight = [[jnp.zeros((CH, 128), WIDE) for _ in range(3)] for _ in range(3)]
        sum_own = jnp.zeros((CH, 128), WIDE)
        sum_down = jnp.zeros((CH, 128), WIDE)
        for k in range(PAIRS):
            active = active_s[k, at, :]
            total = None
            for u in range(3):
                for v in range(3):
                    shifted = near[k][2 - u][2 - v]
                    term = taps[u][v] * shifted
                    total = term if total is None else total + term
                    weight[u][v] = weight[u][v] + shifted * active
            slope = total * gate_s[k, at, :]
            sum_own = sum_own + slope * proj[k, at, :].astype(WIDE)
            sum_down = sum_down + slope * pooled[k, at, :]
            pooled_back[k, at, :] = (scale_down * slope).astype(HALF)
            own_back[k, at, :] = (scale_own * slope).astype(HALF)
        for u in range(3):
            for v in range(3):
                grad_kern[at, 3 * u + v : 3 * u + v + 1] = lane_sum(weight[u][v])
        sums[0] += sum_own
        sums[1] += sum_down

    def accumulate(total, term):
        return term if total is None else total + term

    point, point_f, lat = None, None, None
    for k in range(PAIRS):
        point = accumulate(point, nn(depth_s[k], cotan[k]))
        point_f = accumulate(point_f, nt(pooled_depth[k], pooled_back[k]))
        lat = accumulate(lat, nn(own_back[k], coarse[k]))
        quarter_back[k] = (0.25 * nn(point_fine[...], pooled_back[k])).astype(HALF)
    grad_point[...] = point
    grad_point_fine[...] = point_f
    grad_lat[...] = lat


def backward_kernel(
    coef, cotan, point, quarter_back, act, steep, depth, fine, coarse, lat_fine, lat_coarse,
    kern, up, pool, part_point, part_lat,
    grad_point, grad_lat_fine, grad_lat_coarse, grad_kern, sums,
    back, slope_s,
):
    for s in range(ROWS // 2):
        both = nn(
            jnp.concatenate([point[...], quarter_back[s // 2]], axis=1),
            jnp.concatenate(
                [jnp.concatenate([cotan[2 * s], cotan[2 * s + 1]], axis=1), up[s % 2]], axis=0
            ),
        )
        back[2 * s] = both[:, :128]
        back[2 * s + 1] = both[:, 128:]

    @pl.loop(0, FB // CH)
    def _(step):
        start = pl.multiple_of(step * CH, CH)
        at = pl.ds(start, CH)
        taps = taps_of(kern, start)
        lane = lanes((CH, 128))
        weight = [[None] * 3 for _ in range(3)]
        sides = {}
        for r in range(ROWS + 1):
            if r < ROWS:
                sides[r] = side_fine(back[r, at, :], lane)
            if r >= 1:
                active = act[r - 1, at, :].astype(WIDE)
                total = None
                for u in range(3):
                    if r - u not in sides:
                        continue
                    for v in range(3):
                        shifted = sides[r - u][2 - v]
                        term = taps[u][v] * shifted
                        total = term if total is None else total + term
                        more = active * shifted
                        weight[u][v] = more if weight[u][v] is None else weight[u][v] + more
                slope_s[r - 1, at, :] = (total * steep[r - 1, at, :].astype(WIDE)).astype(HALF)
                sides.pop(r - 2, None)
        for u in range(3):
            for v in range(3):
                grad_kern[at, 3 * u + v : 3 * u + v + 1] = lane_sum(weight[u][v])

    def accumulate(total, term):
        return term if total is None else total + term

    point_g, lat_f, lat_c = None, None, None
    for k in range(PAIRS):
        pooled = []
        for a in range(2):
            s = 2 * k + a
            two = jnp.concatenate([slope_s[2 * s], slope_s[2 * s + 1]], axis=1)
            lat_f = accumulate(
                lat_f, nt(two, jnp.concatenate([fine[2 * s], fine[2 * s + 1]], axis=1))
            )
            point_g = accumulate(
                point_g,
                nt(
                    jnp.concatenate([depth[2 * s], depth[2 * s + 1]], axis=1),
                    jnp.concatenate([cotan[2 * s], cotan[2 * s + 1]], axis=1),
                ),
            )
            pooled.append(two)
        lat_c = accumulate(
            lat_c, nn(nn(jnp.concatenate(pooled, axis=1), pool[...]).astype(HALF), coarse[k])
        )
    grad_point[...] = point_g + part_point[...]
    grad_lat_fine[...] = coef[6] * lat_f
    grad_lat_coarse[...] = coef[7] * lat_c + part_lat[...]
    first = jnp.sum(lat_f * lat_fine[...].astype(WIDE), axis=0, keepdims=True)
    second = jnp.sum(lat_c * lat_coarse[...].astype(WIDE), axis=0, keepdims=True)
    row = lax.broadcasted_iota(jnp.int32, (8, 128), 0)
    sums[0] = jnp.where(row == 0, jnp.sum(first), jnp.where(row == 1, jnp.sum(second), 0.0))


def shaped(*shape, dtype=WIDE):
    return jax.ShapeDtypeStruct(shape, dtype)


def params(kind=None):
    return pltpu.CompilerParams(vmem_limit_bytes=LIMIT, dimension_semantics=kind)


SMEM = pl.BlockSpec(memory_space=pltpu.SMEM)


def whole(*shape):
    return pl.BlockSpec(shape, lambda j: (0,) * len(shape))


def rows_at(count):
    return pl.BlockSpec((count, FB, 128), lambda j: (0, j, 0))


def cols_at(width):
    return pl.BlockSpec((FB, width), lambda j: (j, 0))


def forward(coef, fine, coarse, lat_fine, lat_coarse, kern):
    return pl.pallas_call(
        forward_kernel,
        name="forward",
        grid=(F // FB,),
        in_specs=[
            SMEM, whole(ROWS, 80, 128), whole(1024, 224), cols_at(80), cols_at(224), cols_at(9),
            whole(128, 256), whole(512, 128),
        ],
        out_specs=[rows_at(ROWS), rows_at(ROWS), rows_at(ROWS), rows_at(PAIRS), rows_at(PAIRS)],
        out_shape=[shaped(ROWS, F, 128, dtype=HALF)] * 3 + [shaped(PAIRS, F, 128, dtype=HALF)] * 2,
        scratch_shapes=[
            pltpu.VMEM((ROWS, FB, 128), WIDE),
            pltpu.VMEM((ROWS // 2, FB, 128), WIDE),
        ],
        compiler_params=params(("arbitrary",)),
        cost_estimate=pl.CostEstimate(flops=10**9, bytes_accessed=12 * 10**6, transcendentals=10**6),
    )(
        coef, fine, coarse, lat_fine, lat_coarse, kern,
        jnp.asarray(upsampler(), HALF), jnp.asarray(pooler(0.25), HALF),
    )


def coarse_node(coef, pooled_depth, proj, point_fine, point_coarse, cotan, coarse, kern):
    return pl.pallas_call(
        coarse_kernel,
        name="coarse_node",
        in_specs=[SMEM] + [pl.BlockSpec(memory_space=pltpu.VMEM)] * 8,
        out_specs=[pl.BlockSpec(memory_space=pltpu.VMEM)] * 6,
        out_shape=[
            shaped(F, F), shaped(F, 9), shaped(F, F), shaped(PAIRS, F, 128, dtype=HALF),
            shaped(F, 224), shaped(2, CH, 128),
        ],
        scratch_shapes=[pltpu.VMEM((PAIRS, F, 128), WIDE)] * 4
        + [pltpu.VMEM((PAIRS, F, 128), HALF)] * 3,
        compiler_params=params(),
        cost_estimate=pl.CostEstimate(flops=10**9, bytes_accessed=5 * 10**6, transcendentals=10**6),
    )(
        coef, pooled_depth, proj, point_fine, point_fine.T, point_coarse,
        cotan.reshape(PAIRS, 128, F), coarse.reshape(PAIRS, 128, 224), kern,
    )


def backward(
    coef, cotan, point, quarter_back, act, steep, depth, fine, coarse, lat_fine, lat_coarse,
    kern, part_point, part_lat,
):
    return pl.pallas_call(
        backward_kernel,
        name="backward",
        grid=(F // FB,),
        in_specs=[
            SMEM, whole(ROWS, F, 128), cols_at(F), rows_at(PAIRS), rows_at(ROWS), rows_at(ROWS),
            rows_at(ROWS), whole(ROWS, 80, 128), whole(PAIRS, 128, 224), cols_at(80),
            cols_at(224), cols_at(9), whole(2, 128, 256), whole(512, 128), cols_at(F),
            cols_at(224),
        ],
        out_specs=[
            cols_at(F), cols_at(80), cols_at(224), cols_at(9),
            pl.BlockSpec((1, 8, 128), lambda j: (j, 0, 0)),
        ],
        out_shape=[shaped(F, F), shaped(F, 80), shaped(F, 224), shaped(F, 9), shaped(F // FB, 8, 128)],
        scratch_shapes=[
            pltpu.VMEM((ROWS, FB, 128), WIDE),
            pltpu.VMEM((ROWS, FB, 128), HALF),
        ],
        compiler_params=params(("arbitrary",)),
        cost_estimate=pl.CostEstimate(flops=3 * 10**9, bytes_accessed=16 * 10**6, transcendentals=0),
    )(
        coef, cotan, point, quarter_back, act, steep, depth, fine,
        coarse.reshape(PAIRS, 128, 224), lat_fine, lat_coarse, kern,
        jnp.asarray(upsampler_rows(), HALF), jnp.asarray(pooler(1.0), HALF), part_point, part_lat,
    )


def to_images(values):
    return lax.all_to_all(values, "space", split_axis=0, concat_axis=0, tiled=True)


def thirds(values):
    high = values.astype(HALF)
    rest = values - high.astype(WIDE)
    middle = rest.astype(HALF)
    return jnp.concatenate([high, middle, (rest - middle.astype(WIDE)).astype(HALF)])


def total_over_devices(parts):
    flat = jnp.concatenate([p.astype(HALF).reshape(-1) for p in parts])
    count = lax.axis_size("dp") * lax.axis_size("space")
    share = -(-flat.size // (count * 128)) * 128
    flat = jnp.pad(flat, (0, count * share - flat.size)).reshape(count, share // 128, 128)
    mine = lax.all_to_all(flat, ALL, split_axis=0, concat_axis=0, tiled=True)
    mine = jnp.sum(mine.astype(WIDE), axis=0).astype(HALF)
    mine = jnp.broadcast_to(mine[None], (count,) + mine.shape)
    mine = lax.optimization_barrier(mine)
    full = lax.all_to_all(mine, ALL, split_axis=0, concat_axis=0, tiled=True).reshape(-1)
    out, start = [], 0
    for p in parts:
        out.append(full[start : start + p.size].reshape(p.shape).astype(WIDE))
        start += p.size
    return out


def body(
    fine_map,
    coarse_map,
    fine_cotan,
    coarse_cotan,
    lateral_fine,
    lateral_coarse,
    point_fine,
    point_coarse,
    kernel_fine,
    kernel_coarse,
    joining,
):
    fine_total = joining[0] + joining[1] + EPSILON
    coarse_total = joining[2] + joining[3] + EPSILON
    ratio = joining / jnp.stack([fine_total, fine_total, coarse_total, coarse_total])
    coef = jnp.concatenate([ratio, ratio[2:], ratio[:2]])
    coarse = to_images(jnp.transpose(coarse_map, (0, 2, 3, 1)).reshape(16, 64, 224))
    fine = to_images(jnp.transpose(fine_map, (0, 2, 1, 3))).reshape(ROWS, 80, 128)
    cotan = to_images(jnp.transpose(fine_cotan, (0, 2, 1, 3))).reshape(ROWS, F, 128)
    coarse_cot = jnp.transpose(coarse_cotan, (0, 2, 3, 1)).reshape(1024, F)
    coarse = coarse.reshape(1024, 224)
    lat_fine, lat_coarse = lateral_fine.T, lateral_coarse.T
    kern_fine = kernel_fine.reshape(9, F).T
    kern_coarse = kernel_coarse.reshape(9, F).T
    act, steep, depth, proj_coarse, pooled_depth = forward(
        coef, fine, coarse, lat_fine, lat_coarse, kern_fine
    )
    grad_point_coarse, grad_kern_coarse, part_point, quarter_back, part_lat, sums_coarse = (
        coarse_node(
            coef, pooled_depth, proj_coarse, point_fine, point_coarse, coarse_cot, coarse,
            kern_coarse,
        )
    )
    grad_point_fine, grad_lat_fine, grad_lat_coarse, grad_kern_fine, sums_fine = backward(
        coef, cotan, point_fine, quarter_back, act, steep, depth, fine, coarse, lat_fine,
        lat_coarse, kern_fine, part_point, part_lat,
    )
    sums = jnp.concatenate([sums_fine[:, :2, 0].sum(axis=0), sums_coarse.sum(axis=(1, 2))])
    mean_fine = ratio[0] * sums[0] + ratio[1] * sums[1]
    mean_coarse = ratio[2] * sums[2] + ratio[3] * sums[3]
    join_term = jnp.concatenate(
        [(sums[:2] - mean_fine) / fine_total, (sums[2:] - mean_coarse) / coarse_total]
    )
    early = total_over_devices([grad_point_coarse, grad_kern_coarse])
    late = total_over_devices(
        [grad_point_fine, grad_lat_fine, grad_lat_coarse, grad_kern_fine, thirds(join_term)]
    )
    grad_joining = late[4].reshape(3, 4).sum(axis=0)
    return (
        late[1].T,
        late[2].T,
        late[0],
        early[0],
        late[3].T.reshape(3, 3, F),
        early[1].T.reshape(3, 3, F),
        grad_joining,
    )


def solution(mesh):
    return jax.shard_map(
        body,
        mesh=mesh,
        in_specs=(
            P("dp", None, "space", None),
            P("dp", None, "space", None),
            P("dp", None, "space", None),
            P(("dp", "space"), None, None, None),
            P(),
            P(),
            P(),
            P(),
            P(),
            P(),
            P(),
        ),
        out_specs=(P(), P(), P(), P(), P(), P(), P()),
        check_vma=False,
    )
```

```python
import jax
import jax.numpy as jnp
import numpy as np
from jax import lax
from jax.experimental.layout import Layout, with_layout_constraint
from jax.experimental import pallas as pl
from jax.experimental.pallas import tpu as pltpu
from jax.sharding import Mesh, PartitionSpec as P

EPSILON = 0.0001
F = 384
FB = 128
CH = 16
ROWS = 32
PAIRS = 8
HALF = jnp.bfloat16
WIDE = jnp.float32
CHIPS = ("group", "space")
HALF_ROWS = 1792
ROW_MAJOR = Layout(major_to_minor=(0, 1, 2, 3))
LIMIT = 50 * 1024 * 1024


def nn(left, right):
    return lax.dot_general(left, right, (((1,), (0,)), ((), ())), preferred_element_type=WIDE)


def nt(left, right):
    return lax.dot_general(left, right, (((1,), (1,)), ((), ())), preferred_element_type=WIDE)


def upsampler():
    out = np.zeros((128, 256), np.float32)
    for col in range(128):
        out[col, 2 * col] = 1.0
        out[col, 2 * col + 1] = 1.0
    return out


def upsampler_rows():
    one = upsampler()
    out = np.zeros((2, 128, 256), np.float32)
    for odd in range(2):
        half = one[:, 128 * odd : 128 * odd + 128]
        out[odd, :, :128] = half
        out[odd, :, 128:] = half
    return out


def pooler(scale):
    one = upsampler()
    out = np.zeros((512, 128), np.float32)
    for row in range(4):
        out[128 * row : 128 * row + 128] = one[:, 128 * (row // 2) : 128 * (row // 2) + 128].T
    return out * scale


def lanes(shape):
    return lax.broadcasted_iota(jnp.int32, shape, 1)


def side_fine(cells, lane):
    before = jnp.where(lane == 0, 0.0, pltpu.roll(cells, 1, 1))
    after = jnp.where(lane == 127, 0.0, pltpu.roll(cells, 127, 1))
    return before, cells, after


def side_coarse(cells, lane):
    before = jnp.where((lane % 64) == 0, 0.0, pltpu.roll(cells, 1, 1))
    after = jnp.where((lane % 64) == 63, 0.0, pltpu.roll(cells, 127, 1))
    return before, cells, after


def taps_of(ref, start):
    return [
        [
            jnp.broadcast_to(ref[pl.ds(start, CH), 3 * u + v : 3 * u + v + 1], (CH, 128))
            for v in range(3)
        ]
        for u in range(3)
    ]


def lane_sum(values):
    return jnp.sum(values, axis=1, keepdims=True)


def sigmoid(values):
    return 1.0 / (1.0 + jnp.exp(-values))


def fine_pair(maps, s):
    return maps[s, :80]


def coarse_pair(maps, k):
    return jnp.concatenate([maps[2 * k, 80:144], maps[2 * k + 1, 80:144]], axis=0)


def forward_kernel(
    coef, maps, lat_fine, lat_coarse, kern, up, pool,
    act_out, slope_out, depth_out, proj_out, pooled_out, proj, lifted,
):
    for k in range(PAIRS):
        pair = nt(lat_coarse[...], coarse_pair(maps, k)).astype(HALF)
        proj_out[k] = pair
        both = nn(pair, up[...])
        lifted[2 * k] = both[:, :128]
        lifted[2 * k + 1] = both[:, 128:]
    for s in range(ROWS // 2):
        both = nn(lat_fine[...], fine_pair(maps, s))
        proj[2 * s] = both[:, :128]
        proj[2 * s + 1] = both[:, 128:]
    own, above = coef[0], coef[1]

    @pl.loop(0, FB // CH)
    def _(step):
        start = pl.multiple_of(step * CH, CH)
        at = pl.ds(start, CH)
        taps = taps_of(kern, start)
        lane = lanes((CH, 128))
        sides = {}
        for r in range(ROWS + 1):
            if r < ROWS:
                joined = own * proj[r, at, :] + above * lifted[r // 2, at, :]
                gate = sigmoid(joined)
                active = joined * gate
                act_out[r, at, :] = active.astype(HALF)
                slope_out[r, at, :] = (gate * (1.0 + joined * (1.0 - gate))).astype(HALF)
                sides[r] = side_fine(active, lane)
            if r >= 1:
                total = None
                for u in range(3):
                    if r - 2 + u not in sides:
                        continue
                    for v in range(3):
                        term = taps[u][v] * sides[r - 2 + u][v]
                        total = term if total is None else total + term
                depth_out[r - 1, at, :] = total.astype(HALF)
                sides.pop(r - 2, None)

    for k in range(PAIRS):
        four = jnp.concatenate([depth_out[4 * k + a] for a in range(4)], axis=1)
        pooled_out[k] = nn(four, pool[...]).astype(HALF)


def coarse_kernel(
    coef, pooled_depth, proj, point_fine, point_fine_t, point_coarse, cotan, maps, kern,
    packed, grad_point_fine, quarter_back, grad_lat, sums,
    grad_kern, pooled, active_s, gate_s, back_s, depth_s, pooled_back, own_back,
):
    own, down = coef[2], coef[3]
    for k in range(PAIRS):
        pooled[k] = nn(point_fine_t[...], pooled_depth[k]).astype(HALF).astype(WIDE)
        back_s[k] = nt(point_coarse[...], cotan[k]).astype(HALF).astype(WIDE)
    sums[...] = jnp.zeros_like(sums)
    grad_kern[...] = jnp.zeros_like(grad_kern)

    def rows_of(cells, lane):
        turned = [pltpu.roll(c, 64, 1) for c in cells]
        low = lane < 64
        nil = jnp.zeros((CH, 128), WIDE)
        out = []
        for k in range(PAIRS):
            above = jnp.where(low, turned[k - 1] if k else nil, turned[k])
            below = jnp.where(low, turned[k], turned[k + 1] if k + 1 < PAIRS else nil)
            out.append([side_coarse(c, lane) for c in (above, cells[k], below)])
        return out

    @pl.loop(0, F // CH)
    def _(step):
        start = pl.multiple_of(step * CH, CH)
        at = pl.ds(start, CH)
        taps = taps_of(kern, start)
        lane = lanes((CH, 128))
        active, steep = [], []
        for k in range(PAIRS):
            joined = own * proj[k, at, :].astype(WIDE) + down * pooled[k, at, :]
            gate = sigmoid(joined)
            active.append(joined * gate)
            gate_s[k, at, :] = gate * (1.0 + joined * (1.0 - gate))
        near = rows_of(active, lane)
        for k in range(PAIRS):
            active_s[k, at, :] = active[k]
            total = None
            for u in range(3):
                for v in range(3):
                    term = taps[u][v] * near[k][u][v]
                    total = term if total is None else total + term
            depth_s[k, at, :] = total.astype(HALF)

    @pl.loop(0, F // CH)
    def _(step):
        start = pl.multiple_of(step * CH, CH)
        at = pl.ds(start, CH)
        taps = taps_of(kern, start)
        lane = lanes((CH, 128))
        near = rows_of([back_s[k, at, :] for k in range(PAIRS)], lane)
        weight = [[jnp.zeros((CH, 128), WIDE) for _ in range(3)] for _ in range(3)]
        sum_own = jnp.zeros((CH, 128), WIDE)
        sum_down = jnp.zeros((CH, 128), WIDE)
        for k in range(PAIRS):
            active = active_s[k, at, :]
            total = None
            for u in range(3):
                for v in range(3):
                    shifted = near[k][2 - u][2 - v]
                    term = taps[u][v] * shifted
                    total = term if total is None else total + term
                    weight[u][v] = weight[u][v] + shifted * active
            slope = total * gate_s[k, at, :]
            sum_own = sum_own + slope * proj[k, at, :].astype(WIDE)
            sum_down = sum_down + slope * pooled[k, at, :]
            pooled_back[k, at, :] = (down * slope).astype(HALF)
            own_back[k, at, :] = (own * slope).astype(HALF)
        for u in range(3):
            for v in range(3):
                grad_kern[at, 3 * u + v : 3 * u + v + 1] = lane_sum(weight[u][v])
        sums[0] += sum_own
        sums[1] += sum_down

    def accumulate(total, term):
        return term if total is None else total + term

    point, point_f, lat = None, None, None
    for k in range(PAIRS):
        point = accumulate(point, nn(depth_s[k], cotan[k]))
        point_f = accumulate(point_f, nt(pooled_depth[k], pooled_back[k]))
        lat = accumulate(lat, nn(own_back[k], coarse_pair(maps, k)))
        quarter_back[k] = (0.25 * nn(point_fine[...], pooled_back[k])).astype(HALF)
    for j in range(F // 128):
        packed[F * j : F * j + F] = point[:, 128 * j : 128 * j + 128].astype(HALF)
        taps = grad_kern[128 * j : 128 * j + 128].T[:16]
        packed[3 * F + 16 * j : 3 * F + 16 * j + 16] = taps.astype(HALF)
    grad_point_fine[...] = point_f
    grad_lat[...] = lat


def backward_kernel(
    core, coef, cotan, point, quarter_back, act, steep, depth, maps, lat_fine, lat_coarse,
    kern, up, pool, part_point, part_lat, packed_coarse, sums_coarse,
    keep, send,
    sums, packed, grad_kern, back, slope_s,
):
    j = pl.program_id(0)
    grad_kern[...] = jnp.zeros_like(grad_kern)
    for s in range(ROWS // 2):
        both = nn(
            jnp.concatenate([point[...], quarter_back[s // 2]], axis=1),
            jnp.concatenate(
                [jnp.concatenate([cotan[2 * s], cotan[2 * s + 1]], axis=1), up[s % 2]], axis=0
            ),
        )
        back[2 * s] = both[:, :128]
        back[2 * s + 1] = both[:, 128:]

    @pl.loop(0, FB // CH)
    def _(step):
        start = pl.multiple_of(step * CH, CH)
        at = pl.ds(start, CH)
        taps = taps_of(kern, start)
        lane = lanes((CH, 128))
        weight = [[None] * 3 for _ in range(3)]
        sides = {}
        for r in range(ROWS + 1):
            if r < ROWS:
                sides[r] = side_fine(back[r, at, :], lane)
            if r >= 1:
                active = act[r - 1, at, :].astype(WIDE)
                total = None
                for u in range(3):
                    if r - u not in sides:
                        continue
                    for v in range(3):
                        shifted = sides[r - u][2 - v]
                        term = taps[u][v] * shifted
                        total = term if total is None else total + term
                        more = active * shifted
                        weight[u][v] = more if weight[u][v] is None else weight[u][v] + more
                slope_s[r - 1, at, :] = (total * steep[r - 1, at, :].astype(WIDE)).astype(HALF)
                sides.pop(r - 2, None)
        for u in range(3):
            for v in range(3):
                grad_kern[at, 3 * u + v : 3 * u + v + 1] = lane_sum(weight[u][v])

    def accumulate(total, term):
        return term if total is None else total + term

    point_g, lat_f, lat_c = None, None, None
    for k in range(PAIRS):
        pooled = []
        for a in range(2):
            s = 2 * k + a
            two = jnp.concatenate([slope_s[2 * s], slope_s[2 * s + 1]], axis=1)
            lat_f = accumulate(lat_f, nt(two, fine_pair(maps, s)))
            point_g = accumulate(
                point_g,
                nt(
                    jnp.concatenate([depth[2 * s], depth[2 * s + 1]], axis=1),
                    jnp.concatenate([cotan[2 * s], cotan[2 * s + 1]], axis=1),
                ),
            )
            pooled.append(two)
        lat_c = accumulate(
            lat_c,
            nn(nn(jnp.concatenate(pooled, axis=1), pool[...]).astype(HALF), coarse_pair(maps, k)),
        )
    point_g = (point_g + part_point[...]).astype(HALF)
    for o in range(F // 128):
        packed[128 * o : 128 * o + 128] = point_g[:, 128 * o : 128 * o + 128]
    wide_f = jnp.concatenate([coef[0] * lat_f, jnp.zeros((FB, 48), WIDE)], axis=1)
    packed[384:464] = wide_f.T[:80].astype(HALF)
    packed[464:688] = (coef[1] * lat_c + part_lat[...]).T[:224].astype(HALF)
    packed[688:704] = grad_kern[...].T[:16].astype(HALF)
    first = jnp.sum(lat_f * lat_fine[...].astype(WIDE), axis=0, keepdims=True)
    second = jnp.sum(lat_c * lat_coarse[...].astype(WIDE), axis=0, keepdims=True)
    total_first = jnp.sum(first) + jnp.where(j == 0, 0.0, sums[0])
    total_second = jnp.sum(second) + jnp.where(j == 0, 0.0, sums[1])
    sums[0] = total_first
    sums[1] = total_second

    def put(half, start, values):
        at = pl.ds(start, values.shape[0])

        @pl.when(core[0] == half)
        def _():
            keep[at] = values

        @pl.when(core[0] != half)
        def _():
            send[at] = values

    put(
        jnp.where(j == F // FB - 1, 1, 0),
        pl.multiple_of(jnp.where(j == 1, 704, 0), 16),
        packed[...],
    )

    @pl.when(j == 0)
    def _():
        put(0, 1408, packed_coarse[:F])
        put(1, 704, packed_coarse[F:])

    @pl.when(j == F // FB - 1)
    def _():
        terms = [total_first, total_second, jnp.sum(sums_coarse[0]), jnp.sum(sums_coarse[1])]
        mean_fine = coef[0] * terms[0] + coef[1] * terms[1]
        mean_coarse = coef[2] * terms[2] + coef[3] * terms[3]
        terms = [
            (terms[0] - mean_fine) * coef[4],
            (terms[1] - mean_fine) * coef[4],
            (terms[2] - mean_coarse) * coef[5],
            (terms[3] - mean_coarse) * coef[5],
        ]
        lane = lanes((16, 128))
        row = jnp.zeros((16, 128), WIDE)
        for i, term in enumerate(terms):
            row = jnp.where(lane == i, term, row)
        high = row.astype(HALF).astype(WIDE)
        middle = (row - high).astype(HALF).astype(WIDE)
        low = row - high - middle
        row = high + pltpu.roll(middle, 4, 1) + pltpu.roll(low, 8, 1)
        put(1, 1520, row.astype(HALF))
        put(1, 1536, jnp.zeros((256, 128), HALF))


def shaped(*shape, dtype=WIDE):
    return jax.ShapeDtypeStruct(shape, dtype)


def params(kind=None):
    return pltpu.CompilerParams(vmem_limit_bytes=LIMIT, dimension_semantics=kind)


SMEM = pl.BlockSpec(memory_space=pltpu.SMEM)


def whole(*shape):
    return pl.BlockSpec(shape, lambda j: (0,) * len(shape))


def rows_at(count):
    return pl.BlockSpec((count, FB, 128), lambda j: (0, j, 0))


def cols_at(width):
    return pl.BlockSpec((FB, width), lambda j: (j, 0))


def forward(coef, maps, lat_fine, lat_coarse, kern):
    return pl.pallas_call(
        forward_kernel,
        name="forward",
        grid=(F // FB,),
        in_specs=[
            SMEM, whole(16, 144, 256), cols_at(80), cols_at(256), cols_at(9), whole(128, 256),
            whole(512, 128),
        ],
        out_specs=[rows_at(ROWS), rows_at(ROWS), rows_at(ROWS), rows_at(PAIRS), rows_at(PAIRS)],
        out_shape=[shaped(ROWS, F, 128, dtype=HALF)] * 3 + [shaped(PAIRS, F, 128, dtype=HALF)] * 2,
        scratch_shapes=[
            pltpu.VMEM((ROWS, FB, 128), WIDE),
            pltpu.VMEM((ROWS // 2, FB, 128), WIDE),
        ],
        compiler_params=params(("arbitrary",)),
        cost_estimate=pl.CostEstimate(flops=10**9, bytes_accessed=12 * 10**6, transcendentals=10**6),
    )(
        coef, maps, lat_fine, lat_coarse, kern,
        jnp.asarray(upsampler(), HALF), jnp.asarray(pooler(0.25), HALF),
    )


def coarse_node(coef, pooled_depth, proj, point_fine, point_coarse, cotan, maps, kern):
    return pl.pallas_call(
        coarse_kernel,
        name="coarse_node",
        in_specs=[SMEM] + [pl.BlockSpec(memory_space=pltpu.VMEM)] * 8,
        out_specs=[pl.BlockSpec(memory_space=pltpu.VMEM)] * 5,
        out_shape=[
            shaped(3 * F + 48, 128, dtype=HALF), shaped(F, F),
            shaped(PAIRS, F, 128, dtype=HALF), shaped(F, 256), shaped(2, CH, 128),
        ],
        scratch_shapes=[pltpu.VMEM((F, 128), WIDE)]
        + [pltpu.VMEM((PAIRS, F, 128), WIDE)] * 4
        + [pltpu.VMEM((PAIRS, F, 128), HALF)] * 3,
        compiler_params=params(),
        cost_estimate=pl.CostEstimate(flops=10**9, bytes_accessed=5 * 10**6, transcendentals=10**6),
    )(
        coef, pooled_depth, proj, point_fine, point_fine.T, point_coarse,
        cotan.reshape(PAIRS, 128, F), maps, kern,
    )


def backward(
    core, coef, cotan, point, quarter_back, act, steep, depth, maps, lat_fine, lat_coarse, kern,
    part_point, part_lat, packed_coarse, sums_coarse,
):
    return pl.pallas_call(
        backward_kernel,
        name="backward",
        grid=(F // FB,),
        in_specs=[
            SMEM, SMEM, whole(ROWS, F, 128), cols_at(F), rows_at(PAIRS), rows_at(ROWS),
            rows_at(ROWS), rows_at(ROWS), whole(16, 144, 256), cols_at(80), cols_at(256),
            cols_at(9), whole(2, 128, 256), whole(512, 128), cols_at(F), cols_at(256),
            whole(3 * F + 48, 128), whole(2, CH, 128),
        ],
        out_specs=[whole(HALF_ROWS, 128)] * 2,
        out_shape=[shaped(HALF_ROWS, 128, dtype=HALF)] * 2,
        scratch_shapes=[
            pltpu.SMEM((2,), WIDE),
            pltpu.VMEM((704, 128), HALF),
            pltpu.VMEM((FB, 128), WIDE),
            pltpu.VMEM((ROWS, FB, 128), WIDE),
            pltpu.VMEM((ROWS, FB, 128), HALF),
        ],
        compiler_params=params(("arbitrary",)),
        cost_estimate=pl.CostEstimate(flops=3 * 10**9, bytes_accessed=16 * 10**6, transcendentals=0),
    )(
        core, coef, cotan, point, quarter_back, act, steep, depth, maps, lat_fine, lat_coarse,
        kern, jnp.asarray(upsampler_rows(), HALF), jnp.asarray(pooler(1.0), HALF), part_point,
        part_lat, packed_coarse, sums_coarse,
    )


def unpack_kernel(
    core, mine, other, lat_fine, lat_coarse, point_fine, point_coarse, kern_fine, kern_coarse, join,
):
    def spread(halves):
        for j in range(F // FB):
            at = slice(128 * j, 128 * j + 128)
            rows, base = (halves[1], 0) if j == 2 else (halves[0], 704 * j)
            for o in range(3):
                low = base + 128 * o
                point_fine[at, 128 * o : 128 * o + 128] = rows[low : low + 128].astype(WIDE)
            lat_fine[:, at] = rows[base + 384 : base + 464].astype(WIDE)
            lat_coarse[:, at] = rows[base + 464 : base + 688].astype(WIDE)
            fine_taps = rows[base + 688 : base + 704].astype(WIDE)
            low = 1472 + 16 * j
            coarse_taps = halves[1][low : low + 16].astype(WIDE)
            for u in range(3):
                kern_fine[u, :, at] = fine_taps[3 * u : 3 * u + 3]
                kern_coarse[u, :, at] = coarse_taps[3 * u : 3 * u + 3]
            rows, low = (halves[1], 704 + F * (j - 1)) if j else (halves[0], 1408)
            point_coarse[:, at] = rows[low : low + F].astype(WIDE)
        last = halves[1][1520:1536].astype(WIDE)
        join[...] = (last + pltpu.roll(last, 124, 1) + pltpu.roll(last, 120, 1))[:8]

    @pl.when(core[0] == 0)
    def _():
        spread((mine, other))

    @pl.when(core[0] != 0)
    def _():
        spread((other, mine))


def unpack(core, mine, other):
    return pl.pallas_call(
        unpack_kernel,
        name="unpack",
        in_specs=[SMEM] + [pl.BlockSpec(memory_space=pltpu.VMEM)] * 2,
        out_shape=[
            shaped(80, F), shaped(224, F), shaped(F, F), shaped(F, F), shaped(3, 3, F),
            shaped(3, 3, F), shaped(8, 128),
        ],
        compiler_params=params(),
    )(core, mine, other)


def to_images(values):
    return lax.all_to_all(values, "space", split_axis=0, concat_axis=0, tiled=True)


def to_other_core(values):
    return lax.ppermute(values, "core", [(0, 1), (1, 0)])


def sum_over_devices(keep, send):
    count = lax.axis_size("group") * lax.axis_size("space")
    share = HALF_ROWS // (2 * count)
    both = (keep.astype(WIDE) + to_other_core(send).astype(WIDE)).astype(HALF)
    mine = lax.all_to_all(both.reshape(count, share, 2, 128), CHIPS, 0, 0, tiled=True)
    mine = lax.optimization_barrier(jnp.sum(mine.astype(WIDE), axis=0)).astype(HALF)
    mine = lax.optimization_barrier(jnp.broadcast_to(mine[None], (count,) + mine.shape))
    mine = lax.all_to_all(mine, CHIPS, 0, 0, tiled=True).reshape(HALF_ROWS, 128)
    return mine, to_other_core(mine)


def body(
    fine_map,
    coarse_map,
    fine_cotan,
    coarse_cotan,
    lateral_fine,
    lateral_coarse,
    point_fine,
    point_coarse,
    kernel_fine,
    kernel_coarse,
    joining,
):
    fine_total = joining[0] + joining[1] + EPSILON
    coarse_total = joining[2] + joining[3] + EPSILON
    ratio = joining / jnp.stack([fine_total, fine_total, coarse_total, coarse_total])
    coef = jnp.concatenate([ratio, jnp.stack([1.0 / fine_total, 1.0 / coarse_total])])
    core = lax.axis_index("core").astype(jnp.int32)[None]
    fine = fine_map.reshape(16, 80, 256)
    coarse = jnp.transpose(coarse_map, (0, 2, 3, 1)).reshape(16, 64, 224)
    maps = to_images(jnp.concatenate([fine, jnp.pad(coarse, ((0, 0), (0, 0), (0, 32)))], axis=1))
    cotan = with_layout_constraint(jnp.transpose(fine_cotan, (0, 2, 1, 3)), ROW_MAJOR)
    maps, cotan = lax.optimization_barrier((maps, cotan))
    cotan = to_images(cotan).reshape(ROWS, F, 128)
    coarse_cot = jnp.transpose(coarse_cotan, (0, 2, 3, 1)).reshape(1024, F)
    lat_fine = lateral_fine.T
    lat_coarse = jnp.pad(lateral_coarse.T, ((0, 0), (0, 32)))
    kern_fine = kernel_fine.reshape(9, F).T
    kern_coarse = kernel_coarse.reshape(9, F).T
    act, steep, depth, proj_coarse, pooled_depth = forward(
        coef, maps, lat_fine, lat_coarse, kern_fine
    )
    packed_coarse, part_point, quarter_back, part_lat, sums_coarse = coarse_node(
        coef, pooled_depth, proj_coarse, point_fine, point_coarse, coarse_cot, maps, kern_coarse
    )
    keep, send = backward(
        core, coef, cotan, point_fine, quarter_back, act, steep, depth, maps, lat_fine,
        lat_coarse, kern_fine, part_point, part_lat, packed_coarse, sums_coarse,
    )
    out = unpack(core, *sum_over_devices(keep, send))
    return (*out[:6], out[6][0, :4])


def solution(mesh):
    dp, space = mesh.devices.shape
    finer = Mesh(mesh.devices.reshape(dp // 2, 2, space), ("group", "core", "space"))
    dp = ("group", "core")
    return jax.shard_map(
        body,
        mesh=finer,
        in_specs=(
            P(dp, None, "space", None),
            P(dp, None, "space", None),
            P(dp, None, "space", None),
            P((*dp, "space"), None, None, None),
            P(),
            P(),
            P(),
            P(),
            P(),
            P(),
            P(),
        ),
        out_specs=(P(), P(), P(), P(), P(), P(), P()),
        check_vma=False,
    )
```

```python
import jax
import jax.numpy as jnp
import numpy as np
from jax import lax
from jax.experimental.layout import Layout, with_layout_constraint
from jax.experimental import pallas as pl
from jax.experimental.pallas import tpu as pltpu
from jax.sharding import Mesh, PartitionSpec as P

EPSILON = 0.0001
F = 384
FB = 128
CH = 16
ROWS = 32
PAIRS = 8
HALF = jnp.bfloat16
WIDE = jnp.float32
SPACE = ("z", "y")
LEVEL = ("group", "y")
HALF_ROWS = 1792
ROW_MAJOR = Layout(major_to_minor=(0, 1, 2, 3))
LIMIT = 50 * 1024 * 1024


def nn(left, right):
    return lax.dot_general(left, right, (((1,), (0,)), ((), ())), preferred_element_type=WIDE)


def nt(left, right):
    return lax.dot_general(left, right, (((1,), (1,)), ((), ())), preferred_element_type=WIDE)


def upsampler():
    out = np.zeros((128, 256), np.float32)
    for col in range(128):
        out[col, 2 * col] = 1.0
        out[col, 2 * col + 1] = 1.0
    return out


def upsampler_rows():
    one = upsampler()
    out = np.zeros((2, 128, 256), np.float32)
    for odd in range(2):
        half = one[:, 128 * odd : 128 * odd + 128]
        out[odd, :, :128] = half
        out[odd, :, 128:] = half
    return out


def pooler(scale):
    one = upsampler()
    out = np.zeros((512, 128), np.float32)
    for row in range(4):
        out[128 * row : 128 * row + 128] = one[:, 128 * (row // 2) : 128 * (row // 2) + 128].T
    return out * scale


def lanes(shape):
    return lax.broadcasted_iota(jnp.int32, shape, 1)


def side_fine(cells, lane):
    before = jnp.where(lane == 0, 0.0, pltpu.roll(cells, 1, 1))
    after = jnp.where(lane == 127, 0.0, pltpu.roll(cells, 127, 1))
    return before, cells, after


def side_coarse(cells, lane):
    before = jnp.where((lane % 64) == 0, 0.0, pltpu.roll(cells, 1, 1))
    after = jnp.where((lane % 64) == 63, 0.0, pltpu.roll(cells, 127, 1))
    return before, cells, after


def taps_of(ref, start):
    return [
        [
            jnp.broadcast_to(ref[pl.ds(start, CH), 3 * u + v : 3 * u + v + 1], (CH, 128))
            for v in range(3)
        ]
        for u in range(3)
    ]


def lane_sum(values):
    return jnp.sum(values, axis=1, keepdims=True)


def sigmoid(values):
    return 1.0 / (1.0 + jnp.exp(-values))


def fine_pair(maps, s):
    return maps[s, :80]


def coarse_pair(maps, k):
    return jnp.concatenate([maps[2 * k, 80:144], maps[2 * k + 1, 80:144]], axis=0)


def join_kernel(fine, coarse, maps):
    for i in range(maps.shape[0]):
        maps[i, :80] = fine[i].reshape(80, 256)
        maps[i, 80:, :128] = coarse[i, :, :128]
        maps[i, 80:, 128:224] = coarse[i, :, 128:]
        maps[i, 80:, 224:] = jnp.zeros((64, 32), HALF)


def forward_kernel(
    coef, maps, lat_fine, lat_coarse, kern, up, pool,
    act_out, slope_out, depth_out, proj_out, pooled_out, proj, lifted,
):
    for k in range(PAIRS):
        pair = nt(lat_coarse[...], coarse_pair(maps, k)).astype(HALF)
        proj_out[k] = pair
        both = nn(pair, up[...])
        lifted[2 * k] = both[:, :128]
        lifted[2 * k + 1] = both[:, 128:]
    for s in range(ROWS // 2):
        both = nn(lat_fine[...], fine_pair(maps, s))
        proj[2 * s] = both[:, :128]
        proj[2 * s + 1] = both[:, 128:]
    own, above = coef[0], coef[1]

    @pl.loop(0, FB // CH)
    def _(step):
        start = pl.multiple_of(step * CH, CH)
        at = pl.ds(start, CH)
        taps = taps_of(kern, start)
        lane = lanes((CH, 128))
        sides = {}
        for r in range(ROWS + 1):
            if r < ROWS:
                joined = own * proj[r, at, :] + above * lifted[r // 2, at, :]
                gate = sigmoid(joined)
                active = joined * gate
                act_out[r, at, :] = active.astype(HALF)
                slope_out[r, at, :] = (gate * (1.0 + joined * (1.0 - gate))).astype(HALF)
                sides[r] = side_fine(active, lane)
            if r >= 1:
                total = None
                for u in range(3):
                    if r - 2 + u not in sides:
                        continue
                    for v in range(3):
                        term = taps[u][v] * sides[r - 2 + u][v]
                        total = term if total is None else total + term
                depth_out[r - 1, at, :] = total.astype(HALF)
                sides.pop(r - 2, None)

    for k in range(PAIRS):
        four = jnp.concatenate([depth_out[4 * k + a] for a in range(4)], axis=1)
        pooled_out[k] = nn(four, pool[...]).astype(HALF)


def coarse_kernel(
    coef, pooled_depth, proj, point_fine, point_fine_t, point_coarse, cotan, maps, kern,
    packed, grad_point_fine, quarter_back, grad_lat, sums,
    grad_kern, pooled, active_s, gate_s, back_s, depth_s, pooled_back, own_back,
):
    own, down = coef[2], coef[3]
    for k in range(PAIRS):
        pooled[k] = nn(point_fine_t[...], pooled_depth[k]).astype(HALF).astype(WIDE)
        back_s[k] = nt(point_coarse[...], cotan[k]).astype(HALF).astype(WIDE)
    sums[...] = jnp.zeros_like(sums)
    grad_kern[...] = jnp.zeros_like(grad_kern)

    def rows_of(cells, lane):
        turned = [pltpu.roll(c, 64, 1) for c in cells]
        low = lane < 64
        nil = jnp.zeros((CH, 128), WIDE)
        out = []
        for k in range(PAIRS):
            above = jnp.where(low, turned[k - 1] if k else nil, turned[k])
            below = jnp.where(low, turned[k], turned[k + 1] if k + 1 < PAIRS else nil)
            out.append([side_coarse(c, lane) for c in (above, cells[k], below)])
        return out

    @pl.loop(0, F // CH)
    def _(step):
        start = pl.multiple_of(step * CH, CH)
        at = pl.ds(start, CH)
        taps = taps_of(kern, start)
        lane = lanes((CH, 128))
        active, steep = [], []
        for k in range(PAIRS):
            joined = own * proj[k, at, :].astype(WIDE) + down * pooled[k, at, :]
            gate = sigmoid(joined)
            active.append(joined * gate)
            gate_s[k, at, :] = gate * (1.0 + joined * (1.0 - gate))
        near = rows_of(active, lane)
        for k in range(PAIRS):
            active_s[k, at, :] = active[k]
            total = None
            for u in range(3):
                for v in range(3):
                    term = taps[u][v] * near[k][u][v]
                    total = term if total is None else total + term
            depth_s[k, at, :] = total.astype(HALF)

    @pl.loop(0, F // CH)
    def _(step):
        start = pl.multiple_of(step * CH, CH)
        at = pl.ds(start, CH)
        taps = taps_of(kern, start)
        lane = lanes((CH, 128))
        near = rows_of([back_s[k, at, :] for k in range(PAIRS)], lane)
        weight = [[jnp.zeros((CH, 128), WIDE) for _ in range(3)] for _ in range(3)]
        sum_own = jnp.zeros((CH, 128), WIDE)
        sum_down = jnp.zeros((CH, 128), WIDE)
        for k in range(PAIRS):
            active = active_s[k, at, :]
            total = None
            for u in range(3):
                for v in range(3):
                    shifted = near[k][2 - u][2 - v]
                    term = taps[u][v] * shifted
                    total = term if total is None else total + term
                    weight[u][v] = weight[u][v] + shifted * active
            slope = total * gate_s[k, at, :]
            sum_own = sum_own + slope * proj[k, at, :].astype(WIDE)
            sum_down = sum_down + slope * pooled[k, at, :]
            pooled_back[k, at, :] = (down * slope).astype(HALF)
            own_back[k, at, :] = (own * slope).astype(HALF)
        for u in range(3):
            for v in range(3):
                grad_kern[at, 3 * u + v : 3 * u + v + 1] = lane_sum(weight[u][v])
        sums[0] += sum_own
        sums[1] += sum_down

    def accumulate(total, term):
        return term if total is None else total + term

    point, point_f, lat = None, None, None
    for k in range(PAIRS):
        point = accumulate(point, nn(depth_s[k], cotan[k]))
        point_f = accumulate(point_f, nt(pooled_depth[k], pooled_back[k]))
        lat = accumulate(lat, nn(own_back[k], coarse_pair(maps, k)))
        quarter_back[k] = (0.25 * nn(point_fine[...], pooled_back[k])).astype(HALF)
    for j in range(F // 128):
        packed[F * j : F * j + F] = point[:, 128 * j : 128 * j + 128].astype(HALF)
        taps = grad_kern[128 * j : 128 * j + 128].T[:16]
        packed[3 * F + 16 * j : 3 * F + 16 * j + 16] = taps.astype(HALF)
    grad_point_fine[...] = point_f
    grad_lat[...] = lat


def backward_kernel(
    core, coef, cotan_far, act_far, steep_far, depth_far, point, quarter_back, maps, lat_fine,
    lat_coarse, kern, up, pool, part_point, part_lat, packed_coarse, sums_coarse,
    keep, send,
    cotan, act, steep, depth, halves, grad_kern, grad_point, back, slope_s, arrived,
):
    quarter = ROWS // 4
    share = F // PAIRS

    def of_cotan(q):
        at = pl.ds(quarter * q, quarter)
        return pltpu.make_async_copy(cotan_far.at[at], cotan.at[at], arrived.at[q])

    def of_step(step):
        at = pl.ds(pl.multiple_of(share * step, 16), share)
        rows = pl.ds(4 * step, 4)
        return [
            pltpu.make_async_copy(act_far.at[:, at], act.at[:, at], arrived.at[4 + step]),
            pltpu.make_async_copy(steep_far.at[:, at], steep.at[:, at], arrived.at[12 + step]),
            pltpu.make_async_copy(depth_far.at[rows], depth.at[rows], arrived.at[20 + step]),
        ]

    for q in range(4):
        of_cotan(q).start()
    for step in range(PAIRS):
        for copy in of_step(step):
            copy.start()
    grad_kern[...] = jnp.zeros_like(grad_kern)
    grad_point[...] = part_point[...]
    halves[0, 1408:] = packed_coarse[:F]
    halves[1, 704:1520] = packed_coarse[F:]
    halves[1, 1536:] = jnp.zeros((256, 128), HALF)

    for s in range(ROWS // 2):
        if 2 * s % quarter == 0:
            of_cotan(2 * s // quarter).wait()
        both = nn(
            jnp.concatenate([point[...], quarter_back[s // 2]], axis=1),
            jnp.concatenate(
                [jnp.concatenate([cotan[2 * s], cotan[2 * s + 1]], axis=1), up[s % 2]], axis=0
            ),
        )
        back[2 * s] = both[:, :128].astype(HALF)
        back[2 * s + 1] = both[:, 128:].astype(HALF)

    @pl.loop(0, PAIRS)
    def _(step):
        for copy in of_step(step):
            copy.wait()
        grad_point[...] += nt(
            jnp.concatenate([depth[4 * step + a] for a in range(4)], axis=1),
            jnp.concatenate([cotan[4 * step + a] for a in range(4)], axis=1),
        )
        lane = lanes((CH, 128))
        first_lane, last_lane = lane == 0, lane == 127
        for part in range(F // (CH * PAIRS)):
            start = pl.multiple_of(step * (F // PAIRS) + part * CH, CH)
            at = pl.ds(start, CH)
            taps = [
                [jnp.where(last_lane, 0.0, left), middle, jnp.where(first_lane, 0.0, right)]
                for left, middle, right in taps_of(kern, start)
            ]
            weight = [[None] * 3 for _ in range(3)]
            sides = {}
            for r in range(ROWS + 1):
                if r < ROWS:
                    cells = back[r, at, :]
                    turned = (pltpu.roll(cells, 127, 1), cells, pltpu.roll(cells, 1, 1))
                    sides[r] = [c.astype(WIDE) for c in turned]
                if r >= 1:
                    active = act[r - 1, at, :].astype(WIDE)
                    total = None
                    for u in range(3):
                        if r - u not in sides:
                            continue
                        for v in range(3):
                            shifted = sides[r - u][v]
                            term = taps[u][v] * shifted
                            total = term if total is None else total + term
                            more = active * shifted
                            weight[u][v] = more if weight[u][v] is None else weight[u][v] + more
                    slope_s[r - 1, at, :] = (total * steep[r - 1, at, :].astype(WIDE)).astype(HALF)
                    sides.pop(r - 2, None)
            for u in range(3):
                cleared = [
                    jnp.where(last_lane, 0.0, weight[u][0]),
                    weight[u][1],
                    jnp.where(first_lane, 0.0, weight[u][2]),
                ]
                for v in range(3):
                    grad_kern[at, 3 * u + v : 3 * u + v + 1] = lane_sum(cleared[v])

    def accumulate(total, term):
        return term if total is None else total + term

    lat_f, lat_c = None, None
    for k in range(PAIRS):
        four = jnp.concatenate([slope_s[4 * k + a] for a in range(4)], axis=1)
        both = jnp.concatenate([fine_pair(maps, 2 * k), fine_pair(maps, 2 * k + 1)], axis=1)
        lat_f = accumulate(lat_f, nt(four, both))
        lat_c = accumulate(lat_c, nn(nn(four, pool[...]).astype(HALF), coarse_pair(maps, k)))
    point_t = grad_point[...].astype(HALF)
    wide_f = jnp.concatenate([coef[0] * lat_f, jnp.zeros((F, 48), WIDE)], axis=1)
    lat_f_t = wide_f.T[:80].astype(HALF)
    lat_c_t = (coef[1] * lat_c + part_lat[...]).T[:224].astype(HALF)
    kern_t = grad_kern[...].T[:16].astype(HALF)
    for j in range(F // 128):
        at = slice(128 * j, 128 * j + 128)
        half, base = (1, 0) if j == 2 else (0, 704 * j)
        for o in range(F // 128):
            low = base + 128 * o
            halves[half, low : low + 128] = point_t[at, 128 * o : 128 * o + 128]
        halves[half, base + 384 : base + 464] = lat_f_t[:, at]
        halves[half, base + 464 : base + 688] = lat_c_t[:, at]
        halves[half, base + 688 : base + 704] = kern_t[:, at]

    terms = [
        jnp.sum(lat_f * lat_fine[...].astype(WIDE)),
        jnp.sum(lat_c * lat_coarse[...].astype(WIDE)),
        jnp.sum(sums_coarse[0]),
        jnp.sum(sums_coarse[1]),
    ]
    mean_fine = coef[0] * terms[0] + coef[1] * terms[1]
    mean_coarse = coef[2] * terms[2] + coef[3] * terms[3]
    terms = [
        (terms[0] - mean_fine) * coef[4],
        (terms[1] - mean_fine) * coef[4],
        (terms[2] - mean_coarse) * coef[5],
        (terms[3] - mean_coarse) * coef[5],
    ]
    lane = lanes((16, 128))
    row = jnp.zeros((16, 128), WIDE)
    for i, term in enumerate(terms):
        row = jnp.where(lane == i, term, row)
    high = row.astype(HALF).astype(WIDE)
    middle = (row - high).astype(HALF).astype(WIDE)
    low = row - high - middle
    row = high + pltpu.roll(middle, 4, 1) + pltpu.roll(low, 8, 1)
    halves[1, 1520:1536] = row.astype(HALF)

    keep[...] = halves[core[0]]
    send[...] = halves[1 - core[0]]


def shaped(*shape, dtype=WIDE):
    return jax.ShapeDtypeStruct(shape, dtype)


def params(kind=None):
    return pltpu.CompilerParams(vmem_limit_bytes=LIMIT, dimension_semantics=kind)


SMEM = pl.BlockSpec(memory_space=pltpu.SMEM)


def whole(*shape):
    return pl.BlockSpec(shape, lambda j: (0,) * len(shape))


def rows_at(count):
    return pl.BlockSpec((count, FB, 128), lambda j: (0, j, 0))


def cols_at(width):
    return pl.BlockSpec((FB, width), lambda j: (j, 0))


def join_maps(fine, coarse):
    step = 4
    return pl.pallas_call(
        join_kernel,
        name="join_maps",
        grid=(16 // step,),
        in_specs=[
            pl.BlockSpec((step, 80, 2, 128), lambda i: (i, 0, 0, 0)),
            pl.BlockSpec((step, 64, 224), lambda i: (i, 0, 0)),
        ],
        out_specs=pl.BlockSpec((step, 144, 256), lambda i: (i, 0, 0)),
        out_shape=shaped(16, 144, 256, dtype=HALF),
        compiler_params=params(("arbitrary",)),
    )(fine, coarse)


def forward(coef, maps, lat_fine, lat_coarse, kern):
    return pl.pallas_call(
        forward_kernel,
        name="forward",
        grid=(F // FB,),
        in_specs=[
            SMEM, whole(16, 144, 256), cols_at(80), cols_at(256), cols_at(9), whole(128, 256),
            whole(512, 128),
        ],
        out_specs=[rows_at(ROWS), rows_at(ROWS), rows_at(ROWS), rows_at(PAIRS), rows_at(PAIRS)],
        out_shape=[shaped(ROWS, F, 128, dtype=HALF)] * 3 + [shaped(PAIRS, F, 128, dtype=HALF)] * 2,
        scratch_shapes=[
            pltpu.VMEM((ROWS, FB, 128), WIDE),
            pltpu.VMEM((ROWS // 2, FB, 128), WIDE),
        ],
        compiler_params=params(("arbitrary",)),
        cost_estimate=pl.CostEstimate(flops=10**9, bytes_accessed=12 * 10**6, transcendentals=10**6),
    )(
        coef, maps, lat_fine, lat_coarse, kern,
        jnp.asarray(upsampler(), HALF), jnp.asarray(pooler(0.25), HALF),
    )


def coarse_node(coef, pooled_depth, proj, point_fine, point_coarse, cotan, maps, kern):
    return pl.pallas_call(
        coarse_kernel,
        name="coarse_node",
        in_specs=[SMEM] + [pl.BlockSpec(memory_space=pltpu.VMEM)] * 8,
        out_specs=[pl.BlockSpec(memory_space=pltpu.VMEM)] * 5,
        out_shape=[
            shaped(3 * F + 48, 128, dtype=HALF), shaped(F, F),
            shaped(PAIRS, F, 128, dtype=HALF), shaped(F, 256), shaped(2, CH, 128),
        ],
        scratch_shapes=[pltpu.VMEM((F, 128), WIDE)]
        + [pltpu.VMEM((PAIRS, F, 128), WIDE)] * 4
        + [pltpu.VMEM((PAIRS, F, 128), HALF)] * 3,
        compiler_params=params(),
        cost_estimate=pl.CostEstimate(flops=10**9, bytes_accessed=5 * 10**6, transcendentals=10**6),
    )(
        coef, pooled_depth, proj, point_fine, point_fine.T, point_coarse,
        cotan.reshape(PAIRS, 128, F), maps, kern,
    )


def backward(
    core, coef, cotan, point, quarter_back, act, steep, depth, maps, lat_fine, lat_coarse, kern,
    part_point, part_lat, packed_coarse, sums_coarse,
):
    far = pl.BlockSpec(memory_space=pl.ANY)
    near = pl.BlockSpec(memory_space=pltpu.VMEM)
    return pl.pallas_call(
        backward_kernel,
        name="backward",
        in_specs=[SMEM, SMEM] + [far] * 4 + [near] * 12,
        out_specs=[near] * 2,
        out_shape=[shaped(HALF_ROWS, 128, dtype=HALF)] * 2,
        scratch_shapes=[
            *[pltpu.VMEM((ROWS, F, 128), HALF)] * 4,
            pltpu.VMEM((2, HALF_ROWS, 128), HALF),
            pltpu.VMEM((F, 128), WIDE),
            pltpu.VMEM((F, F), WIDE),
            pltpu.VMEM((ROWS, F, 128), HALF),
            pltpu.VMEM((ROWS, F, 128), HALF),
            pltpu.SemaphoreType.DMA((28,)),
        ],
        compiler_params=params(),
        cost_estimate=pl.CostEstimate(flops=3 * 10**9, bytes_accessed=16 * 10**6, transcendentals=0),
    )(
        core, coef, cotan, act, steep, depth, point, quarter_back, maps, lat_fine, lat_coarse, kern,
        jnp.asarray(upsampler_rows(), HALF), jnp.asarray(pooler(1.0), HALF), part_point, part_lat,
        packed_coarse, sums_coarse,
    )


def unpack_kernel(
    core, mine, other, lat_fine, lat_coarse, point_fine, point_coarse, kern_fine, kern_coarse, join,
):
    def spread(halves):
        for j in range(F // FB):
            at = slice(128 * j, 128 * j + 128)
            rows, base = (halves[1], 0) if j == 2 else (halves[0], 704 * j)
            for o in range(3):
                low = base + 128 * o
                point_fine[at, 128 * o : 128 * o + 128] = rows[low : low + 128].astype(WIDE)
            lat_fine[:, at] = rows[base + 384 : base + 464].astype(WIDE)
            lat_coarse[:, at] = rows[base + 464 : base + 688].astype(WIDE)
            fine_taps = rows[base + 688 : base + 704].astype(WIDE)
            low = 1472 + 16 * j
            coarse_taps = halves[1][low : low + 16].astype(WIDE)
            for u in range(3):
                kern_fine[u, :, at] = fine_taps[3 * u : 3 * u + 3]
                kern_coarse[u, :, at] = coarse_taps[3 * u : 3 * u + 3]
            rows, low = (halves[1], 704 + F * (j - 1)) if j else (halves[0], 1408)
            point_coarse[:, at] = rows[low : low + F].astype(WIDE)
        last = halves[1][1520:1536].astype(WIDE)
        join[...] = (last + pltpu.roll(last, 124, 1) + pltpu.roll(last, 120, 1))[:8]

    @pl.when(core[0] == 0)
    def _():
        spread((mine, other))

    @pl.when(core[0] != 0)
    def _():
        spread((other, mine))


def unpack(core, mine, other):
    return pl.pallas_call(
        unpack_kernel,
        name="unpack",
        in_specs=[SMEM] + [pl.BlockSpec(memory_space=pltpu.VMEM)] * 2,
        out_shape=[
            shaped(80, F), shaped(224, F), shaped(F, F), shaped(F, F), shaped(3, 3, F),
            shaped(3, 3, F), shaped(8, 128),
        ],
        compiler_params=params(),
    )(core, mine, other)


def to_images(values):
    return lax.all_to_all(values, SPACE, split_axis=0, concat_axis=0, tiled=True)


def to_other_core(values):
    return lax.ppermute(values, "core", [(0, 1), (1, 0)])


def to_all(values, axes):
    count = lax.axis_size(axes)
    copies = lax.optimization_barrier(jnp.broadcast_to(values[None], (count,) + values.shape))
    return lax.all_to_all(copies, axes, 0, 0, tiled=True)


def added(values):
    return lax.optimization_barrier(jnp.sum(values.astype(WIDE), axis=0)).astype(HALF)


def sum_over_devices(keep, send):
    count = lax.axis_size(LEVEL)
    both = (keep.astype(WIDE) + to_other_core(send).astype(WIDE)).astype(HALF)
    shares = both.reshape(count, HALF_ROWS // count, 128)
    mine = added(lax.all_to_all(shares, LEVEL, 0, 0, tiled=True))
    mine = added(to_all(mine, "z"))
    mine = to_all(mine, LEVEL).reshape(HALF_ROWS, 128)
    return mine, to_other_core(mine)


def body(
    fine_map,
    coarse_map,
    fine_cotan,
    coarse_cotan,
    lateral_fine,
    lateral_coarse,
    point_fine,
    point_coarse,
    kernel_fine,
    kernel_coarse,
    joining,
):
    fine_total = joining[0] + joining[1] + EPSILON
    coarse_total = joining[2] + joining[3] + EPSILON
    ratio = joining / jnp.stack([fine_total, fine_total, coarse_total, coarse_total])
    coef = jnp.concatenate([ratio, jnp.stack([1.0 / fine_total, 1.0 / coarse_total])])
    core = lax.axis_index("core").astype(jnp.int32)[None]
    coarse = jnp.transpose(coarse_map, (0, 2, 3, 1)).reshape(16, 64, 224)
    maps = to_images(join_maps(fine_map, coarse))
    cotan = with_layout_constraint(jnp.transpose(fine_cotan, (0, 2, 1, 3)), ROW_MAJOR)
    maps, cotan = lax.optimization_barrier((maps, cotan))
    cotan = to_images(cotan).reshape(ROWS, F, 128)
    coarse_cot = jnp.transpose(coarse_cotan, (0, 2, 3, 1)).reshape(1024, F)
    lat_fine = lateral_fine.T
    lat_coarse = jnp.pad(lateral_coarse.T, ((0, 0), (0, 32)))
    kern_fine = kernel_fine.reshape(9, F).T
    kern_coarse = kernel_coarse.reshape(9, F).T
    act, steep, depth, proj_coarse, pooled_depth = forward(
        coef, maps, lat_fine, lat_coarse, kern_fine
    )
    packed_coarse, part_point, quarter_back, part_lat, sums_coarse = coarse_node(
        coef, pooled_depth, proj_coarse, point_fine, point_coarse, coarse_cot, maps, kern_coarse
    )
    keep, send = backward(
        core, coef, cotan, point_fine, quarter_back, act, steep, depth, maps, lat_fine,
        lat_coarse, kern_fine, part_point, part_lat, packed_coarse, sums_coarse,
    )
    out = unpack(core, *sum_over_devices(keep, send))
    return (*out[:6], out[6][0, :4])


def solution(mesh):
    dp, space = mesh.devices.shape
    finer = Mesh(mesh.devices.reshape(dp // 2, 2, space // 2, 2), ("group", "core", "z", "y"))
    dp = ("group", "core")
    return jax.shard_map(
        body,
        mesh=finer,
        in_specs=(
            P(dp, None, SPACE, None),
            P(dp, None, SPACE, None),
            P(dp, None, SPACE, None),
            P((*dp, *SPACE), None, None, None),
            P(),
            P(),
            P(),
            P(),
            P(),
            P(),
            P(),
        ),
        out_specs=(P(), P(), P(), P(), P(), P(), P()),
        check_vma=False,
    )
```

```python
import jax
import jax.numpy as jnp
from jax import lax
from jax.experimental.layout import Layout, with_layout_constraint
from jax.experimental import pallas as pl
from jax.experimental.pallas import tpu as pltpu
from jax.sharding import Mesh, PartitionSpec as P

EPSILON = 0.0001
F = 384
FB = 128
CH = 16
ROWS = 32
PAIRS = 8
HALF = jnp.bfloat16
WIDE = jnp.float32
SPACE = ("z", "y")
LEVEL = ("group", "y")
HALF_ROWS = 1792
ROW_MAJOR = Layout(major_to_minor=(0, 1, 2, 3))
LIMIT = 50 * 1024 * 1024


def nn(left, right):
    return lax.dot_general(left, right, (((1,), (0,)), ((), ())), preferred_element_type=WIDE)


def nt(left, right):
    return lax.dot_general(left, right, (((1,), (1,)), ((), ())), preferred_element_type=WIDE)


def ones_where(condition):
    return jnp.where(condition, 1.0, 0.0).astype(HALF)


def upsampler(rows):
    shape = (128, 256)
    cell = lax.broadcasted_iota(jnp.int32, shape, 0)
    lane = lax.broadcasted_iota(jnp.int32, shape, 1)
    row = jnp.where(lane < 128, rows[0], rows[1])
    return ones_where(cell == 64 * row + ((lane & 127) >> 1))


def pooler():
    shape = (512, 128)
    cell = lax.broadcasted_iota(jnp.int32, shape, 0)
    lane = lax.broadcasted_iota(jnp.int32, shape, 1)
    return ones_where(lane == ((cell >> 8) << 6) + ((cell & 127) >> 1))


def lanes(shape):
    return lax.broadcasted_iota(jnp.int32, shape, 1)


def side_fine(cells, lane):
    before = jnp.where(lane == 0, 0.0, pltpu.roll(cells, 1, 1))
    after = jnp.where(lane == 127, 0.0, pltpu.roll(cells, 127, 1))
    return before, cells, after


def side_coarse(cells, lane):
    before = jnp.where((lane % 64) == 0, 0.0, pltpu.roll(cells, 1, 1))
    after = jnp.where((lane % 64) == 63, 0.0, pltpu.roll(cells, 127, 1))
    return before, cells, after


def taps_of(ref, start):
    return [
        [
            jnp.broadcast_to(ref[pl.ds(start, CH), 3 * u + v : 3 * u + v + 1], (CH, 128))
            for v in range(3)
        ]
        for u in range(3)
    ]


def lane_sum(values):
    return jnp.sum(values, axis=1, keepdims=True)


def sigmoid(values):
    return 1.0 / (1.0 + jnp.exp(-values))


def fine_pair(maps, s):
    return maps[s, :80]


def coarse_pair(maps, k):
    return jnp.concatenate([maps[2 * k, 80:144], maps[2 * k + 1, 80:144]], axis=0)


def join_kernel(fine_far, coarse_far, maps, fine, coarse, arrived):
    count = maps.shape[0]
    step = count // 8
    copies = []
    for q in range(8):
        at = pl.ds(step * q, step)
        copies.append(pltpu.make_async_copy(fine_far.at[at], fine.at[at], arrived.at[q]))
        copies.append(pltpu.make_async_copy(coarse_far.at[at], coarse.at[at], arrived.at[8 + q]))
    for copy in copies:
        copy.start()
    for i in range(count):
        if i % step == 0:
            copies[2 * i // step].wait()
            copies[2 * i // step + 1].wait()
        maps[i, :80] = fine[i].reshape(80, 256)
        maps[i, 80:, :128] = coarse[i, :, :128]
        maps[i, 80:, 128:224] = coarse[i, :, 128:]
        maps[i, 80:, 224:] = jnp.zeros((64, 32), HALF)


def forward_kernel(
    coef, maps, lat_fine, lat_coarse, kern,
    act_out, slope_out, turned_out, proj_out, pooled_out, proj, lifted, depth,
):
    up, pool = upsampler((0, 1)), pooler()
    for k in range(PAIRS):
        pair = nt(lat_coarse[...], coarse_pair(maps, k)).astype(HALF)
        proj_out[k] = pair
        both = nn(pair, up)
        lifted[2 * k] = both[:, :128]
        lifted[2 * k + 1] = both[:, 128:]
    for s in range(ROWS // 2):
        both = nn(lat_fine[...], fine_pair(maps, s))
        proj[2 * s] = both[:, :128]
        proj[2 * s + 1] = both[:, 128:]
    own, above = coef[0], coef[1]

    @pl.loop(0, FB // CH)
    def _(step):
        start = pl.multiple_of(step * CH, CH)
        at = pl.ds(start, CH)
        taps = taps_of(kern, start)
        lane = lanes((CH, 128))
        sides = {}
        for r in range(ROWS + 1):
            if r < ROWS:
                joined = own * proj[r, at, :] + above * lifted[r // 2, at, :]
                gate = sigmoid(joined)
                active = joined * gate
                act_out[r, at, :] = active.astype(HALF)
                slope_out[r, at, :] = (gate * (1.0 + joined * (1.0 - gate))).astype(HALF)
                sides[r] = side_fine(active, lane)
            if r >= 1:
                total = None
                for u in range(3):
                    if r - 2 + u not in sides:
                        continue
                    for v in range(3):
                        term = taps[u][v] * sides[r - 2 + u][v]
                        total = term if total is None else total + term
                depth[r - 1, at, :] = total.astype(HALF)
                sides.pop(r - 2, None)

    for k in range(PAIRS):
        four = jnp.concatenate([depth[4 * k + a] for a in range(4)], axis=1)
        pooled_out[k] = (0.25 * nn(four, pool)).astype(HALF)
    for r in range(ROWS):
        turned_out[128 * r : 128 * r + 128] = depth[r].T


def coarse_kernel(
    coef, pooled_depth, proj, point_fine, point_fine_t, point_coarse, cotan, maps, kern,
    packed, grad_point_fine, quarter_back, grad_lat, sums,
    grad_kern, pooled, active_s, gate_s, back_s, depth_s, pooled_back, own_back,
):
    own, down = coef[2], coef[3]
    for k in range(PAIRS):
        pooled[k] = nn(point_fine_t[...], pooled_depth[k]).astype(HALF).astype(WIDE)
        back_s[k] = nt(point_coarse[...], cotan[k]).astype(HALF).astype(WIDE)
    sums[...] = jnp.zeros_like(sums)
    grad_kern[...] = jnp.zeros_like(grad_kern)

    def rows_of(cells, lane):
        turned = [pltpu.roll(c, 64, 1) for c in cells]
        low = lane < 64
        nil = jnp.zeros((CH, 128), WIDE)
        out = []
        for k in range(PAIRS):
            above = jnp.where(low, turned[k - 1] if k else nil, turned[k])
            below = jnp.where(low, turned[k], turned[k + 1] if k + 1 < PAIRS else nil)
            out.append([side_coarse(c, lane) for c in (above, cells[k], below)])
        return out

    @pl.loop(0, F // CH)
    def _(step):
        start = pl.multiple_of(step * CH, CH)
        at = pl.ds(start, CH)
        taps = taps_of(kern, start)
        lane = lanes((CH, 128))
        active, steep = [], []
        for k in range(PAIRS):
            joined = own * proj[k, at, :].astype(WIDE) + down * pooled[k, at, :]
            gate = sigmoid(joined)
            active.append(joined * gate)
            gate_s[k, at, :] = gate * (1.0 + joined * (1.0 - gate))
        near = rows_of(active, lane)
        for k in range(PAIRS):
            active_s[k, at, :] = active[k]
            total = None
            for u in range(3):
                for v in range(3):
                    term = taps[u][v] * near[k][u][v]
                    total = term if total is None else total + term
            depth_s[k, at, :] = total.astype(HALF)

    @pl.loop(0, F // CH)
    def _(step):
        start = pl.multiple_of(step * CH, CH)
        at = pl.ds(start, CH)
        taps = taps_of(kern, start)
        lane = lanes((CH, 128))
        near = rows_of([back_s[k, at, :] for k in range(PAIRS)], lane)
        weight = [[jnp.zeros((CH, 128), WIDE) for _ in range(3)] for _ in range(3)]
        sum_own = jnp.zeros((CH, 128), WIDE)
        sum_down = jnp.zeros((CH, 128), WIDE)
        for k in range(PAIRS):
            active = active_s[k, at, :]
            total = None
            for u in range(3):
                for v in range(3):
                    shifted = near[k][2 - u][2 - v]
                    term = taps[u][v] * shifted
                    total = term if total is None else total + term
                    weight[u][v] = weight[u][v] + shifted * active
            slope = total * gate_s[k, at, :]
            sum_own = sum_own + slope * proj[k, at, :].astype(WIDE)
            sum_down = sum_down + slope * pooled[k, at, :]
            pooled_back[k, at, :] = (down * slope).astype(HALF)
            own_back[k, at, :] = (own * slope).astype(HALF)
        for u in range(3):
            for v in range(3):
                grad_kern[at, 3 * u + v : 3 * u + v + 1] = lane_sum(weight[u][v])
        sums[0] += sum_own
        sums[1] += sum_down

    def accumulate(total, term):
        return term if total is None else total + term

    point, point_f, lat = None, None, None
    for k in range(PAIRS):
        point = accumulate(point, nn(depth_s[k], cotan[k]))
        point_f = accumulate(point_f, nt(pooled_back[k], pooled_depth[k]))
        lat = accumulate(lat, nn(own_back[k], coarse_pair(maps, k)))
        quarter_back[k] = (0.25 * nn(point_fine[...], pooled_back[k])).astype(HALF)
    for j in range(F // 128):
        packed[F * j : F * j + F] = point[:, 128 * j : 128 * j + 128].astype(HALF)
        taps = grad_kern[128 * j : 128 * j + 128].T[:16]
        packed[3 * F + 16 * j : 3 * F + 16 * j + 16] = taps.astype(HALF)
    grad_point_fine[...] = point_f
    grad_lat[...] = lat


def backward_kernel(
    core, coef, cotan_far, act_far, steep_far, depth_far, maps_far, point, quarter_back, lat_fine,
    lat_coarse, kern, part_point, part_lat, packed_coarse, sums_coarse,
    keep, send,
    cotan, act, steep, depth, maps, halves, grad_kern, grad_point, back, slope_s, arrived,
):
    quarter = ROWS // 8
    share = F // PAIRS

    def of_cotan(q):
        at = pl.ds(quarter * q, quarter)
        return pltpu.make_async_copy(cotan_far.at[at], cotan.at[at], arrived.at[q])

    def of_step(step):
        at = pl.ds(pl.multiple_of(share * step, 16), share)
        rows = pl.ds(pl.multiple_of(512 * step, 512), 512)
        return [
            pltpu.make_async_copy(act_far.at[:, at], act.at[:, at], arrived.at[8 + step]),
            pltpu.make_async_copy(steep_far.at[:, at], steep.at[:, at], arrived.at[16 + step]),
            pltpu.make_async_copy(depth_far.at[rows], depth.at[rows], arrived.at[24 + step]),
        ]

    for q in range(8):
        of_cotan(q).start()
    for step in range(PAIRS):
        for copy in of_step(step):
            copy.start()
    of_maps = pltpu.make_async_copy(maps_far, maps, arrived.at[32])
    of_maps.start()
    grad_kern[...] = jnp.zeros_like(grad_kern)
    grad_point[...] = part_point[...]
    halves[0, 1408:] = packed_coarse[:F]
    halves[1, 704:1520] = packed_coarse[F:]
    halves[1, 1536:] = jnp.zeros((256, 128), HALF)

    up, pool = [upsampler((odd, odd)) for odd in range(2)], pooler()
    for s in range(ROWS // 2):
        if 2 * s % quarter == 0:
            of_cotan(2 * s // quarter).wait()
        both = nn(
            jnp.concatenate([point[...], quarter_back[s // 2]], axis=1),
            jnp.concatenate(
                [jnp.concatenate([cotan[2 * s], cotan[2 * s + 1]], axis=1), up[s % 2]], axis=0
            ),
        )
        back[2 * s] = both[:, :128].astype(HALF)
        back[2 * s + 1] = both[:, 128:].astype(HALF)

    @pl.loop(0, PAIRS)
    def _(step):
        for copy in of_step(step):
            copy.wait()
        grad_point[...] += nn(
            jnp.concatenate([cotan[4 * step + a] for a in range(4)], axis=1),
            depth[pl.ds(pl.multiple_of(512 * step, 512), 512)],
        )
        lane = lanes((CH, 128))
        first_lane, last_lane = lane == 0, lane == 127
        for part in range(F // (CH * PAIRS)):
            start = pl.multiple_of(step * (F // PAIRS) + part * CH, CH)
            at = pl.ds(start, CH)
            taps = [
                [jnp.where(last_lane, 0.0, left), middle, jnp.where(first_lane, 0.0, right)]
                for left, middle, right in taps_of(kern, start)
            ]
            weight = [[None] * 3 for _ in range(3)]
            totals, actives = {}, {}
            for r in range(ROWS + 1):
                if r < ROWS:
                    actives[r] = act[r, at, :].astype(WIDE)
                if r >= 1:
                    q = r - 1
                    cells = back[q, at, :]
                    turned = (pltpu.roll(cells, 127, 1), cells, pltpu.roll(cells, 1, 1))
                    near = [c.astype(WIDE) for c in turned]
                    for u in range(3):
                        i = q - 1 + u
                        if i not in actives:
                            continue
                        for v in range(3):
                            term = taps[u][v] * near[v]
                            totals[i] = term if i not in totals else totals[i] + term
                            more = actives[i] * near[v]
                            weight[u][v] = more if weight[u][v] is None else weight[u][v] + more
                    done = [q - 1] if r < ROWS else [q - 1, q]
                    for i in done:
                        if i >= 0:
                            gate = steep[i, at, :].astype(WIDE)
                            slope_s[i, at, :] = (totals.pop(i) * gate).astype(HALF)
                            actives.pop(i)
            for u in range(3):
                cleared = [
                    jnp.where(last_lane, 0.0, weight[u][0]),
                    weight[u][1],
                    jnp.where(first_lane, 0.0, weight[u][2]),
                ]
                for v in range(3):
                    grad_kern[at, 3 * u + v : 3 * u + v + 1] = lane_sum(cleared[v])

    def accumulate(total, term):
        return term if total is None else total + term

    of_maps.wait()
    lat_f, lat_c = None, None
    for k in range(PAIRS):
        four = jnp.concatenate([slope_s[4 * k + a] for a in range(4)], axis=1)
        both = jnp.concatenate([fine_pair(maps, 2 * k), fine_pair(maps, 2 * k + 1)], axis=1)
        lat_f = accumulate(lat_f, nt(four, both))
        lat_c = accumulate(lat_c, nn(nn(four, pool).astype(HALF), coarse_pair(maps, k)))
    point_t = grad_point[...].T.astype(HALF)
    wide_f = jnp.concatenate([coef[0] * lat_f, jnp.zeros((F, 48), WIDE)], axis=1)
    lat_f_t = wide_f.T[:80].astype(HALF)
    lat_c_t = (coef[1] * lat_c + part_lat[...]).T[:224].astype(HALF)
    kern_t = grad_kern[...].T[:16].astype(HALF)
    for j in range(F // 128):
        at = slice(128 * j, 128 * j + 128)
        half, base = (1, 0) if j == 2 else (0, 704 * j)
        for o in range(F // 128):
            low = base + 128 * o
            halves[half, low : low + 128] = point_t[at, 128 * o : 128 * o + 128]
        halves[half, base + 384 : base + 464] = lat_f_t[:, at]
        halves[half, base + 464 : base + 688] = lat_c_t[:, at]
        halves[half, base + 688 : base + 704] = kern_t[:, at]

    terms = [
        jnp.sum(lat_f * lat_fine[...].astype(WIDE)),
        jnp.sum(lat_c * lat_coarse[...].astype(WIDE)),
        jnp.sum(sums_coarse[0]),
        jnp.sum(sums_coarse[1]),
    ]
    mean_fine = coef[0] * terms[0] + coef[1] * terms[1]
    mean_coarse = coef[2] * terms[2] + coef[3] * terms[3]
    terms = [
        (terms[0] - mean_fine) * coef[4],
        (terms[1] - mean_fine) * coef[4],
        (terms[2] - mean_coarse) * coef[5],
        (terms[3] - mean_coarse) * coef[5],
    ]
    lane = lanes((16, 128))
    row = jnp.zeros((16, 128), WIDE)
    for i, term in enumerate(terms):
        row = jnp.where(lane == i, term, row)
    high = row.astype(HALF).astype(WIDE)
    middle = (row - high).astype(HALF).astype(WIDE)
    low = row - high - middle
    row = high + pltpu.roll(middle, 4, 1) + pltpu.roll(low, 8, 1)
    halves[1, 1520:1536] = row.astype(HALF)

    keep[...] = halves[core[0]]
    send[...] = halves[1 - core[0]]


def shaped(*shape, dtype=WIDE):
    return jax.ShapeDtypeStruct(shape, dtype)


def params(kind=None):
    return pltpu.CompilerParams(vmem_limit_bytes=LIMIT, dimension_semantics=kind)


SMEM = pl.BlockSpec(memory_space=pltpu.SMEM)


def whole(*shape):
    return pl.BlockSpec(shape, lambda j: (0,) * len(shape))


def rows_at(count):
    return pl.BlockSpec((count, FB, 128), lambda j: (0, j, 0))


def cols_at(width):
    return pl.BlockSpec((FB, width), lambda j: (j, 0))


def join_maps(fine, coarse):
    return pl.pallas_call(
        join_kernel,
        name="join_maps",
        in_specs=[pl.BlockSpec(memory_space=pl.ANY)] * 2,
        out_specs=pl.BlockSpec(memory_space=pltpu.VMEM),
        out_shape=shaped(16, 144, 256, dtype=HALF),
        scratch_shapes=[
            pltpu.VMEM((16, 80, 2, 128), HALF),
            pltpu.VMEM((16, 64, 224), HALF),
            pltpu.SemaphoreType.DMA((16,)),
        ],
        compiler_params=pltpu.CompilerParams(vmem_limit_bytes=60 * 1024 * 1024),
    )(fine, coarse)


def forward(coef, maps, lat_fine, lat_coarse, kern):
    return pl.pallas_call(
        forward_kernel,
        name="forward",
        grid=(F // FB,),
        in_specs=[
            SMEM, whole(16, 144, 256), cols_at(80), cols_at(256), cols_at(9),
        ],
        out_specs=[
            rows_at(ROWS), rows_at(ROWS), pl.BlockSpec((ROWS * 128, FB), lambda j: (0, j)),
            rows_at(PAIRS), rows_at(PAIRS),
        ],
        out_shape=[shaped(ROWS, F, 128, dtype=HALF)] * 2
        + [shaped(ROWS * 128, F, dtype=HALF)]
        + [shaped(PAIRS, F, 128, dtype=HALF)] * 2,
        scratch_shapes=[
            pltpu.VMEM((ROWS, FB, 128), WIDE),
            pltpu.VMEM((ROWS // 2, FB, 128), WIDE),
            pltpu.VMEM((ROWS, FB, 128), HALF),
        ],
        compiler_params=params(("arbitrary",)),
        cost_estimate=pl.CostEstimate(flops=10**9, bytes_accessed=12 * 10**6, transcendentals=10**6),
    )(
        coef, maps, lat_fine, lat_coarse, kern,
    )


def coarse_node(coef, pooled_depth, proj, point_fine, point_coarse, cotan, maps, kern):
    return pl.pallas_call(
        coarse_kernel,
        name="coarse_node",
        in_specs=[SMEM] + [pl.BlockSpec(memory_space=pltpu.VMEM)] * 8,
        out_specs=[pl.BlockSpec(memory_space=pltpu.VMEM)] * 5,
        out_shape=[
            shaped(3 * F + 48, 128, dtype=HALF), shaped(F, F),
            shaped(PAIRS, F, 128, dtype=HALF), shaped(F, 256), shaped(2, CH, 128),
        ],
        scratch_shapes=[pltpu.VMEM((F, 128), WIDE)]
        + [pltpu.VMEM((PAIRS, F, 128), WIDE)] * 4
        + [pltpu.VMEM((PAIRS, F, 128), HALF)] * 3,
        compiler_params=params(),
        cost_estimate=pl.CostEstimate(flops=10**9, bytes_accessed=5 * 10**6, transcendentals=10**6),
    )(
        coef, pooled_depth, proj, point_fine, point_fine.T, point_coarse,
        cotan.reshape(PAIRS, 128, F), maps, kern,
    )


def backward(
    core, coef, cotan, point, quarter_back, act, steep, depth, maps, lat_fine, lat_coarse, kern,
    part_point, part_lat, packed_coarse, sums_coarse,
):
    far = pl.BlockSpec(memory_space=pl.ANY)
    near = pl.BlockSpec(memory_space=pltpu.VMEM)
    return pl.pallas_call(
        backward_kernel,
        name="backward",
        in_specs=[SMEM, SMEM] + [far] * 5 + [near] * 9,
        out_specs=[near] * 2,
        out_shape=[shaped(HALF_ROWS, 128, dtype=HALF)] * 2,
        scratch_shapes=[
            *[pltpu.VMEM((ROWS, F, 128), HALF)] * 3,
            pltpu.VMEM((ROWS * 128, F), HALF),
            pltpu.VMEM((16, 144, 256), HALF),
            pltpu.VMEM((2, HALF_ROWS, 128), HALF),
            pltpu.VMEM((F, 128), WIDE),
            pltpu.VMEM((F, F), WIDE),
            pltpu.VMEM((ROWS, F, 128), HALF),
            pltpu.VMEM((ROWS, F, 128), HALF),
            pltpu.SemaphoreType.DMA((33,)),
        ],
        compiler_params=params(),
        cost_estimate=pl.CostEstimate(flops=3 * 10**9, bytes_accessed=16 * 10**6, transcendentals=0),
    )(
        core, coef, cotan, act, steep, depth, maps, point, quarter_back, lat_fine, lat_coarse, kern,
        part_point, part_lat, packed_coarse, sums_coarse,
    )


def unpack_kernel(
    core, mine, other, lat_fine, lat_coarse, point_fine, point_coarse, kern_fine, kern_coarse, join,
):
    def spread(halves):
        for j in range(F // FB):
            at = slice(128 * j, 128 * j + 128)
            rows, base = (halves[1], 0) if j == 2 else (halves[0], 704 * j)
            for o in range(3):
                low = base + 128 * o
                point_fine[at, 128 * o : 128 * o + 128] = rows[low : low + 128].astype(WIDE)
            lat_fine[:, at] = rows[base + 384 : base + 464].astype(WIDE)
            lat_coarse[:, at] = rows[base + 464 : base + 688].astype(WIDE)
            fine_taps = rows[base + 688 : base + 704].astype(WIDE)
            low = 1472 + 16 * j
            coarse_taps = halves[1][low : low + 16].astype(WIDE)
            for u in range(3):
                kern_fine[u, :, at] = fine_taps[3 * u : 3 * u + 3]
                kern_coarse[u, :, at] = coarse_taps[3 * u : 3 * u + 3]
            rows, low = (halves[1], 704 + F * (j - 1)) if j else (halves[0], 1408)
            point_coarse[:, at] = rows[low : low + F].astype(WIDE)
        last = halves[1][1520:1536].astype(WIDE)
        lane = lanes((16, 128))
        first_row = lax.broadcasted_iota(jnp.int32, (16, 128), 0) == 0
        for i in range(4):
            join[i] = jnp.sum(jnp.where(first_row & ((lane & 3) == i) & (lane < 12), last, 0.0))

    @pl.when(core[0] == 0)
    def _():
        spread((mine, other))

    @pl.when(core[0] != 0)
    def _():
        spread((other, mine))


def unpack(core, mine, other):
    return pl.pallas_call(
        unpack_kernel,
        name="unpack",
        in_specs=[SMEM] + [pl.BlockSpec(memory_space=pltpu.VMEM)] * 2,
        out_shape=[
            shaped(80, F), shaped(224, F), shaped(F, F), shaped(F, F), shaped(3, 3, F),
            shaped(3, 3, F), shaped(4),
        ],
        out_specs=[pl.BlockSpec(memory_space=pltpu.VMEM)] * 6 + [SMEM],
        compiler_params=params(),
    )(core, mine, other)


def to_images(values):
    return lax.all_to_all(values, SPACE, split_axis=0, concat_axis=0, tiled=True)


def to_other_core(values):
    return lax.ppermute(values, "core", [(0, 1), (1, 0)])


def to_all(values, axes):
    count = lax.axis_size(axes)
    copies = lax.optimization_barrier(jnp.broadcast_to(values[None], (count,) + values.shape))
    return lax.all_to_all(copies, axes, 0, 0, tiled=True)


def added(values):
    return lax.optimization_barrier(jnp.sum(values.astype(WIDE), axis=0)).astype(HALF)


def sum_over_devices(keep, send):
    count = lax.axis_size(LEVEL)
    both = (keep.astype(WIDE) + to_other_core(send).astype(WIDE)).astype(HALF)
    shares = both.reshape(count, HALF_ROWS // count, 128)
    mine = added(lax.all_to_all(shares, LEVEL, 0, 0, tiled=True))
    mine = added(to_all(mine, "z"))
    mine = to_all(mine, LEVEL).reshape(HALF_ROWS, 128)
    return mine, to_other_core(mine)


def body(
    fine_map,
    coarse_map,
    fine_cotan,
    coarse_cotan,
    lateral_fine,
    lateral_coarse,
    point_fine,
    point_coarse,
    kernel_fine,
    kernel_coarse,
    joining,
):
    fine_total = joining[0] + joining[1] + EPSILON
    coarse_total = joining[2] + joining[3] + EPSILON
    ratio = joining / jnp.stack([fine_total, fine_total, coarse_total, coarse_total])
    coef = jnp.concatenate([ratio, jnp.stack([1.0 / fine_total, 1.0 / coarse_total])])
    core = lax.axis_index("core").astype(jnp.int32)[None]
    coarse = jnp.transpose(coarse_map, (0, 2, 3, 1)).reshape(16, 64, 224)
    maps = to_images(join_maps(fine_map, coarse))
    cotan = with_layout_constraint(jnp.transpose(fine_cotan, (0, 2, 1, 3)), ROW_MAJOR)
    maps, cotan = lax.optimization_barrier((maps, cotan))
    cotan = to_images(cotan).reshape(ROWS, F, 128)
    coarse_cot = jnp.transpose(coarse_cotan, (0, 2, 3, 1)).reshape(1024, F)
    lat_fine = lateral_fine.T
    lat_coarse = jnp.pad(lateral_coarse.T, ((0, 0), (0, 32)))
    kern_fine = kernel_fine.reshape(9, F).T
    kern_coarse = kernel_coarse.reshape(9, F).T
    act, steep, depth, proj_coarse, pooled_depth = forward(
        coef, maps, lat_fine, lat_coarse, kern_fine
    )
    packed_coarse, part_point, quarter_back, part_lat, sums_coarse = coarse_node(
        coef, pooled_depth, proj_coarse, point_fine, point_coarse, coarse_cot, maps, kern_coarse
    )
    keep, send = backward(
        core, coef, cotan, point_fine, quarter_back, act, steep, depth, maps, lat_fine,
        lat_coarse, kern_fine, part_point, part_lat, packed_coarse, sums_coarse,
    )
    return tuple(unpack(core, *sum_over_devices(keep, send)))


def solution(mesh):
    dp, space = mesh.devices.shape
    finer = Mesh(mesh.devices.reshape(dp // 2, 2, space // 2, 2), ("group", "core", "z", "y"))
    dp = ("group", "core")
    return jax.shard_map(
        body,
        mesh=finer,
        in_specs=(
            P(dp, None, SPACE, None),
            P(dp, None, SPACE, None),
            P(dp, None, SPACE, None),
            P((*dp, *SPACE), None, None, None),
            P(),
            P(),
            P(),
            P(),
            P(),
            P(),
            P(),
        ),
        out_specs=(P(), P(), P(), P(), P(), P(), P()),
        check_vma=False,
    )
```
